32 devices in a mesh: expert: 4 (over y, x), shard: 8 (over z, core).
Axes of the slice: x: 2, y: 2, z: 4, core: 2. Of those that a mesh axis runs over, the one named last changes fastest.
Arguments:
- grad_out: bfloat16 [4, 1024, 3072], P('expert', 'shard'), may hold values from -6 to 6
- gate_pre: bfloat16 [4, 1024, 8192], P('expert', None, 'shard'), may hold values from -8 to 8
- up_pre: bfloat16 [4, 1024, 8192], P('expert', None, 'shard'), may hold values from -6 to 6
- counts: int32 [4, 8], P('expert', 'shard'), may hold values from 32 to 128
- placement: int32 [4], replicated, may hold values from 0 to 63, as said below
- master: float32 [4, 8192, 3072], P('expert', 'shard')
Outputs:
- d_gate: bfloat16 [4, 1024, 8192], P('expert', None, 'shard')
- d_up: bfloat16 [4, 1024, 8192], P('expert', None, 'shard')
- new_master: float32 [4, 8192, 3072], P('expert', 'shard')
The draws below stay inside these ranges and needn't reach their ends.
Inputs may be any that keep to these rules, and one draw needn't show every extreme that they name: `placement`: slots that hold the same expert form aligned blocks of 1, 2 or 4 consecutive slots, each block starting at a multiple of its size; different blocks hold different experts.
All inputs are finite; a program needn't handle non-finite values.
Results may differ from the reference program's by a relative error of at most 0.006.
Values may be sent and summed in bfloat16 or wider, within the bound.
No kernel may reach another device: no remote copies, remote signals or barrier semaphores. Data moves between devices by JAX's collectives and lax.ppermute only.
A program may use at most 256 MiB of HBM per device.

```python
import jax
import jax.numpy as jnp
from jax import lax

D = 3072
FFW = 8192
NEXP = 64
ROW_DEV = 128
SLOTS = 4
ROWS = 1024
N_SHARD = 8


def slot_experts(key):
    base = jax.random.fold_in(key, 3)
    patterns = jnp.array([[0, 0, 0, 0], [0, 0, 2, 2], [0, 0, 2, 3], [0, 1, 2, 2], [0, 1, 2, 3]], jnp.int32)
    blocks = SLOTS // 4
    picked = jax.random.randint(jax.random.fold_in(base, 1), (blocks,), 0, 5)
    leaders = patterns[picked] + 4 * jnp.arange(blocks, dtype=jnp.int32)[:, None]
    labels = jax.random.permutation(jax.random.fold_in(base, 2), NEXP - 1)[:SLOTS].astype(jnp.int32)
    top_block = jax.random.randint(jax.random.fold_in(base, 4), (), 0, blocks)
    labels = jnp.where(jnp.arange(SLOTS, dtype=jnp.int32) == 4 * top_block, NEXP - 1, labels).astype(jnp.int32)
    return labels[leaders.reshape(SLOTS)]


def draw_placement(key, part):
    return slot_experts(key)


def draw_master(key, part):
    labels = slot_experts(key)
    weight_key = jax.random.fold_in(key, 11)
    spread = jnp.float32(FFW) ** (-0.5)

    def one_slot(label):
        slot_key = jax.random.fold_in(weight_key, label)
        values = jax.random.normal(slot_key, (FFW, D), jnp.float32)
        return values * spread
    return jax.vmap(one_slot)(labels)


def set_ends(values, own_key, least, high):
    longest = values.shape.index(max(values.shape))
    spots = []
    for shift in (0, 1):
        where = [jax.random.randint(jax.random.fold_in(own_key, axis), (), 0, length) for axis, length in enumerate(values.shape)]
        where[longest] = (where[longest] + shift) % values.shape[longest]
        spots.append(tuple(where))
    return values.at[spots[0]].set(least).at[spots[1]].set(high)


def block_scale(rng, shape, split, low, high):
    def one(dim, parts):
        heights = jax.random.uniform(jax.random.fold_in(jax.random.fold_in(rng, 6), dim), (parts,), jnp.float32, low / len(split), high / len(split))
        return jnp.repeat(jnp.exp(heights), shape[dim] // parts).reshape((-1,) + (1,) * (len(shape) - dim - 1))

    loudness = one(*split[0])
    for cut in split[1:]:
        loudness = loudness * one(*cut)
    return loudness


def scatter_about(key, dims, deviation, bound, shards=(), held_as=jnp.bfloat16):
    level = block_scale(key, dims, shards, -0.22, 0.18) if shards else 1.0
    values = jax.random.normal(key, dims, jnp.float32) * deviation * level
    return jnp.minimum(jnp.maximum(values, -bound), bound).astype(held_as)


def setup_inputs(seed: int = 0) -> dict:
    splits = jax.random.split(jax.random.key(seed), 7)
    grad_out = scatter_about(splits[0], (SLOTS, ROWS, D), 1.0, 6.0, ((0, 4), (1, 8)))
    gate_pre = scatter_about(splits[1], (SLOTS, ROWS, FFW), 1.5, 8.0, ((0, 4), (2, 8)))
    up_pre = scatter_about(splits[2], (SLOTS, ROWS, FFW), 1.0, 6.0, ((0, 4), (2, 8)))
    counts = set_ends(jax.random.randint(splits[3], (SLOTS, N_SHARD), ROW_DEV // 4, ROW_DEV + 1), jax.random.fold_in(splits[3], 1), ROW_DEV // 4, ROW_DEV).astype(jnp.int32)
    placement = draw_placement(jax.random.fold_in(splits[6], 71), 0)
    master = draw_master(jax.random.fold_in(splits[6], 71), 0)
    return {"grad_out": grad_out, "gate_pre": gate_pre, "up_pre": up_pre, "counts": counts, "placement": placement, "master": master}


learn_rate = 0.02
rms_eps = 1e-06

def swiglu_back(out_grad, gate_pre, up_pre, master):
    weight_work = master.astype(jnp.bfloat16)
    gate_val = gate_pre.astype(jnp.float32)
    up_val = up_pre.astype(jnp.float32)
    gate_sig = jax.nn.sigmoid(gate_val)
    gate_act = gate_val * gate_sig
    d_hidden = lax.dot_general(out_grad, weight_work, (((1,), (1,)), ((), ())), preferred_element_type=jnp.float32)
    d_up = (d_hidden * gate_act).astype(jnp.bfloat16)
    d_gate = (d_hidden * up_val * (gate_sig * (1.0 + gate_val * (1.0 - gate_sig)))).astype(jnp.bfloat16)
    hidden = (gate_act * up_val).astype(jnp.bfloat16)
    weight_grad = lax.dot_general(hidden, out_grad, (((0,), (0,)), ((), ())), preferred_element_type=jnp.float32)
    return (d_gate, d_up, weight_grad)

def reference(grad_out, gate_pre, up_pre, counts, placement, master):
    row_pos = jnp.arange(ROWS, dtype=jnp.int32) % ROW_DEV
    limits = jnp.repeat(counts, ROW_DEV, axis=1)
    row_valid = (row_pos[None, :] < limits).astype(jnp.bfloat16)
    masked = grad_out * row_valid[:, :, None]
    d_gate, d_up, slot_grads = lax.map(lambda items: swiglu_back(*items), (masked, gate_pre, up_pre, master))

    def update(slot_index):
        partner_mask = (placement == placement[slot_index]).astype(jnp.float32)
        grad_sum = jnp.tensordot(partner_mask, slot_grads, axes=1, precision=lax.Precision.HIGHEST)
        row_rms = jnp.sqrt(lax.optimization_barrier(jnp.mean(grad_sum * grad_sum, axis=1, keepdims=True)) + rms_eps)
        return master[slot_index] - learn_rate * grad_sum / row_rms
    new_master = lax.map(update, jnp.arange(SLOTS, dtype=jnp.int32))
    return (d_gate, d_up, new_master)
```

```python
import jax
import jax.numpy as jnp
from jax import lax
from jax.sharding import PartitionSpec as P

learn_rate = 0.02
rms_eps = 1e-06
col_chunks = 3


def shifted(block, step, count):
    if step > 0:
        pairs = [(i, i + step) for i in range(count - step)]
    else:
        pairs = [(i, i + step) for i in range(-step, count)]
    return lax.ppermute(block, "shard", pairs)


def gather_line(block, chip, count):
    chips = count // 2
    ups, downs = [], []
    up = down = block
    for _ in range(chips - 1):
        up = shifted(up, 2, count)
        down = shifted(down, -2, count)
        ups.append(up)
        downs.append(down)
    pieces = jnp.stack(ups[::-1] + [block] + downs)
    return lax.dynamic_slice_in_dim(pieces, chips - 1 - chip, chips, axis=0)


def gather_rows(block, count):
    chip = lax.axis_index("shard") // 2
    mine = gather_line(block, chip, count)
    other = lax.ppermute(mine, "shard", [(i, i ^ 1) for i in range(count)])
    return jnp.stack([mine, other])


def swap_cores(rows, core, count):
    split = rows.reshape(count // 2, 2, -1, rows.shape[-1])
    first = jnp.where(core == 0, split[:, 0], split[:, 1])
    second = jnp.where(core == 0, split[:, 1], split[:, 0])
    return jnp.stack([first, second])


def unswap_cores(rows, core):
    zero = jnp.where(core == 0, rows[0], rows[1])
    one = jnp.where(core == 0, rows[1], rows[0])
    return jnp.stack([zero, one], axis=1).reshape(-1, rows.shape[-1])


def per_device(grad_out, gate_pre, up_pre, counts, placement, master):
    n_slot = lax.axis_size("expert")
    n_shard = lax.axis_size("shard")
    core = lax.axis_index("shard") % 2
    slot = lax.axis_index("expert")
    d_model = grad_out.shape[2]
    width = d_model // col_chunks
    pair_same = placement[0::2] == placement[1::2]
    four_same = placement[0::4] == placement[2::4]
    any_four = jnp.any(four_same)
    all_four = jnp.all(four_same)
    any_pair = jnp.any(pair_same)

    def share(bit):
        return lax.dynamic_index_in_dim(placement, slot ^ bit, keepdims=False) == (
            lax.dynamic_index_in_dim(placement, slot, keepdims=False)
        )

    def body(mode, grad_out, gate_pre, up_pre, counts, placement, master):
        live = jnp.arange(grad_out.shape[1], dtype=jnp.int32) < counts[0, 0]
        masked = jnp.where(live[:, None], grad_out[0], jnp.zeros((), grad_out.dtype))
        rows = masked.shape[0]
        gate_val = gate_pre[0].astype(jnp.float32)
        up_val = up_pre[0].astype(jnp.float32)
        gate_sig = jax.nn.sigmoid(gate_val)
        gate_act = gate_val * gate_sig
        gate_slope = gate_sig * (1.0 + gate_val * (1.0 - gate_sig))
        hidden = (gate_act * up_val).astype(jnp.bfloat16)
        hidden = swap_cores(hidden, core, n_shard)
        if mode == "pair":
            partner = [(i, i ^ 1) for i in range(n_slot)]
            hidden_two = lax.ppermute(hidden, "expert", partner)
            hidden_two = jnp.where(share(1), hidden_two, jnp.zeros((), hidden.dtype))
            hidden = jnp.stack([hidden, hidden_two], axis=2)
        ffw = hidden.shape[-1]
        hidden = hidden.reshape(-1, ffw)
        d_hidden = None
        sums = []
        square = 0.0
        for chunk in range(col_chunks):
            cols = slice(chunk * width, (chunk + 1) * width)
            block = masked[:, cols]
            if mode == "pair":
                block = jnp.concatenate([block, lax.ppermute(block, "expert", partner)])
            whole = gather_rows(block, n_shard)
            own = whole[:, :, :rows].reshape(-1, width)
            whole = whole.reshape(-1, width)
            part = lax.dot_general(
                own, master[0, :, cols].astype(jnp.bfloat16), (((1,), (1,)), ((), ())),
                preferred_element_type=jnp.float32,
            )
            d_hidden = part if d_hidden is None else d_hidden + part
            grad = lax.dot_general(
                hidden, whole, (((0,), (0,)), ((), ())), preferred_element_type=jnp.float32
            )
            if mode == "four":
                groups = None
                if n_slot > 4:
                    groups = [list(range(i, i + 4)) for i in range(0, n_slot, 4)]
                grad = lax.psum(grad.astype(jnp.bfloat16), "expert", axis_index_groups=groups)
                grad = grad.astype(jnp.float32)
            if mode == "mixed":
                for bit in (1, 2):
                    pairs = [(i, i ^ bit) for i in range(n_slot)]
                    got = lax.ppermute(grad.astype(jnp.bfloat16), "expert", pairs)
                    grad = grad + jnp.where(share(bit), got.astype(jnp.float32), 0.0)
            sums.append(grad)
            square = square + jnp.sum(grad * grad, axis=1, keepdims=True)
        d_hidden = unswap_cores(d_hidden.reshape(2, n_shard // 2, rows, ffw), core)
        up_acc = (d_hidden * gate_act).astype(jnp.bfloat16)
        gate_acc = (d_hidden * up_val * gate_slope).astype(jnp.bfloat16)
        scale = learn_rate / jnp.sqrt(square / d_model + rms_eps)
        fresh = [
            master[0, :, i * width : (i + 1) * width] - grad * scale for i, grad in enumerate(sums)
        ]
        return gate_acc[None], up_acc[None], jnp.concatenate(fresh, axis=1)[None]

    modes = ["none", "pair", "four"] + (["mixed"] if n_slot > 4 else [])
    which = jnp.where(any_pair, jnp.where(any_four, jnp.where(all_four, 2, len(modes) - 1), 1), 0)
    return lax.switch(
        which,
        [lambda *a, mode=mode: body(mode, *a) for mode in modes],
        grad_out, gate_pre, up_pre, counts, placement, master,
    )


def solution(mesh):
    return jax.shard_map(
        per_device,
        mesh=mesh,
        in_specs=(
            P("expert", "shard", None),
            P("expert", None, "shard"),
            P("expert", None, "shard"),
            P("expert", "shard"),
            P(),
            P("expert", "shard", None),
        ),
        out_specs=(
            P("expert", None, "shard"),
            P("expert", None, "shard"),
            P("expert", "shard", None),
        ),
        check_vma=False,
    )
```

```python
import functools

import jax
import jax.numpy as jnp
from jax import lax
from jax.experimental import pallas as pl
from jax.experimental.pallas import tpu as pltpu
from jax.sharding import PartitionSpec as P

learn_rate = 0.02
rms_eps = 1e-06
col_chunks = 3
vmem_bytes = 48 * 2**20


def dot(a, b, dims):
    return lax.dot_general(a, b, (dims, ((), ())), preferred_element_type=jnp.float32)


def hidden_kernel(gate_ref, up_ref, out_ref):
    gate = gate_ref[0].astype(jnp.float32)
    hidden = gate * jax.nn.sigmoid(gate) * up_ref[0].astype(jnp.float32)
    out_ref[...] = hidden.T.astype(out_ref.dtype)


def hidden_transposed(gate_pre, up_pre):
    _, rows, ffw = gate_pre.shape
    tall = 256
    block = pl.BlockSpec((1, tall, ffw), lambda i: (0, i, 0))
    return pl.pallas_call(
        hidden_kernel,
        grid=(rows // tall,),
        in_specs=[block, block],
        out_specs=pl.BlockSpec((ffw, tall), lambda i: (0, i)),
        out_shape=jax.ShapeDtypeStruct((ffw, rows), jnp.bfloat16),
        compiler_params=pltpu.CompilerParams(vmem_limit_bytes=vmem_bytes),
        cost_estimate=pl.CostEstimate(
            flops=8 * rows * ffw, bytes_accessed=6 * rows * ffw, transcendentals=rows * ffw
        ),
    )(gate_pre, up_pre)


def update_rows(master, grads, out_ref):
    square = sum(jnp.sum(g * g, axis=1, keepdims=True) for g in grads)
    width = grads[0].shape[1]
    scale = learn_rate / jnp.sqrt(square / (width * len(grads)) + rms_eps)
    for i, grad in enumerate(grads):
        cols = slice(i * width, (i + 1) * width)
        out_ref[0, :, cols] = master[:, cols] - grad * scale


def chunk_kernel(chunk, n_parts, has_acc, gates, n_grads, flag_ref, *refs):
    refs = list(refs)
    own_ref = refs.pop(0)
    own_hidden = refs.pop(0)
    parts = [(refs.pop(0), refs.pop(0)) for _ in range(n_parts)]
    master_ref = refs.pop(0)
    acc_ref = refs.pop(0) if has_acc else None
    gate_ref, up_ref = (refs.pop(0), refs.pop(0)) if gates else (None, None)
    grad_refs = [refs.pop(0) for _ in range(n_grads)]
    own = own_ref[...]
    width = own.shape[1]
    grad = dot(own_hidden[...], own, ((1,), (0,)))
    if parts:
        more = sum(dot(h[...], p[...], ((1,), (0,))) for p, h in parts)
        grad = grad + jnp.where(flag_ref[1] > 0, more, 0.0)
    if n_grads:
        weight = master_ref[0, :, chunk * width : (chunk + 1) * width]
    else:
        weight = master_ref[0]
    d_hidden = dot(own, weight.astype(jnp.bfloat16), ((1,), (1,)))
    if has_acc:
        d_hidden = d_hidden + acc_ref[...]
    if gates:
        gate_out, up_out, out_ref = refs
        gate = gate_ref[0].astype(jnp.float32)
        up = up_ref[0].astype(jnp.float32)
        sig = jax.nn.sigmoid(gate)
        up_out[0] = (d_hidden * (gate * sig)).astype(up_out.dtype)
        slope = sig * (1.0 + gate * (1.0 - sig))
        gate_out[0] = (d_hidden * up * slope).astype(gate_out.dtype)
    else:
        acc_out, out_ref = refs
        acc_out[...] = d_hidden
    if n_grads:
        grads = [ref[...] for ref in grad_refs]
        grads.insert(chunk, grad)
        update_rows(master_ref[0], grads, out_ref)
    else:
        out_ref[...] = grad.astype(out_ref.dtype)


def chunk_call(chunk, flags, own, hidden, master, acc=None, parts=(), gate_up=None, grads=(),
               grad_type=jnp.float32):
    rows, width = own.shape
    ffw = hidden.shape[0]
    tall = 256
    last = gate_up is not None
    specs = [
        pl.BlockSpec((rows, width), lambda i, flag: (0, 0)),
        pl.BlockSpec((tall, rows), lambda i, flag: (i, 0)),
    ]
    args = [own, hidden]
    for rows_part, hidden_part, place in parts:
        deep = rows_part.shape[0]
        specs.append(pl.BlockSpec((deep, width), lambda i, flag: (0, 0)))
        specs.append(pl.BlockSpec((tall, deep), lambda i, flag, place=place: (i, place(flag))))
        args += [rows_part, hidden_part]
    full = pl.BlockSpec((1, tall, master.shape[2]), lambda i, flag: (0, i, 0))
    specs.append(full if grads else pl.BlockSpec((1, tall, width), lambda i, flag: (0, i, chunk)))
    args.append(master)
    acc_spec = pl.BlockSpec((rows, tall), lambda i, flag: (0, i))
    gate_spec = pl.BlockSpec((1, rows, tall), lambda i, flag: (0, 0, i))
    grad_spec = pl.BlockSpec((tall, width), lambda i, flag: (i, 0))
    aliases = {}
    if acc is not None:
        if not last:
            aliases = {1 + len(args): 0}
        specs.append(acc_spec)
        args.append(acc)
    if last:
        specs += [gate_spec, gate_spec]
        args += list(gate_up)
    specs += [grad_spec] * len(grads)
    args += list(grads)
    if last:
        out_specs = [gate_spec, gate_spec]
        out_shape = [jax.ShapeDtypeStruct(a.shape, a.dtype) for a in gate_up]
    else:
        out_specs = [acc_spec]
        out_shape = [jax.ShapeDtypeStruct((rows, ffw), jnp.float32)]
    if grads:
        out_specs.append(full)
        out_shape.append(jax.ShapeDtypeStruct(master.shape, master.dtype))
    else:
        out_specs.append(grad_spec)
        out_shape.append(jax.ShapeDtypeStruct((ffw, width), grad_type))
    deep = 2 * rows + sum(p[0].shape[0] for p in parts)
    return pl.pallas_call(
        functools.partial(
            chunk_kernel, chunk, len(parts), acc is not None, last, len(grads)
        ),
        grid_spec=pltpu.PrefetchScalarGridSpec(
            num_scalar_prefetch=1, grid=(ffw // tall,), in_specs=specs, out_specs=out_specs
        ),
        out_shape=out_shape,
        input_output_aliases=aliases,
        compiler_params=pltpu.CompilerParams(vmem_limit_bytes=vmem_bytes),
        cost_estimate=pl.CostEstimate(
            flops=2 * deep * ffw * width,
            bytes_accessed=16 * ffw * width + (24 * ffw * width if grads else 0),
            transcendentals=0,
        ),
    )(flags, *args)


def update_kernel(master_ref, *refs):
    update_rows(master_ref[0], [r[...].astype(jnp.float32) for r in refs[:-1]], refs[-1])


def update_call(master, grads):
    _, ffw, d_model = master.shape
    tall = 128
    full = pl.BlockSpec((1, tall, d_model), lambda i: (0, i, 0))
    part = pl.BlockSpec((tall, grads[0].shape[1]), lambda i: (i, 0))
    return pl.pallas_call(
        update_kernel,
        grid=(ffw // tall,),
        in_specs=[full] + [part] * len(grads),
        out_specs=full,
        out_shape=jax.ShapeDtypeStruct(master.shape, master.dtype),
        compiler_params=pltpu.CompilerParams(vmem_limit_bytes=vmem_bytes),
        cost_estimate=pl.CostEstimate(
            flops=6 * ffw * d_model, bytes_accessed=10 * ffw * d_model, transcendentals=0
        ),
    )(master, *grads)


def after(value, other):
    return lax.optimization_barrier((value, other))[0]


def per_device(grad_out, gate_pre, up_pre, counts, placement, master):
    n_slot = lax.axis_size("expert")
    n_shard = lax.axis_size("shard")
    core = lax.axis_index("shard") % 2
    slot = lax.axis_index("expert")
    width = grad_out.shape[2] // col_chunks
    order = jnp.arange(n_slot, dtype=jnp.int32)
    same = placement[:, None] == placement[None, :]
    pair_count = jnp.sum(same & (order[:, None] ^ 1 == order[None, :]), dtype=jnp.int32)
    four_count = jnp.sum(same & (order[:, None] ^ 2 == order[None, :]), dtype=jnp.int32)

    def share(bit):
        return jnp.any(same & (order[:, None] == slot) & (order[None, :] == slot ^ bit))

    def body(mode, grad_out, gate_pre, up_pre, counts, placement, master):
        live = jnp.arange(grad_out.shape[1], dtype=jnp.int32) < counts[0, 0]
        masked = jnp.where(live[:, None], grad_out[0], jnp.zeros((), grad_out.dtype))
        hidden = hidden_transposed(gate_pre, up_pre)
        flags = jnp.stack([core, share(1).astype(jnp.int32)])
        gate_up = (gate_pre, up_pre)
        blocks = [masked[:, i * width : (i + 1) * width] for i in range(col_chunks)]
        partner = [(i, i ^ 1) for i in range(n_slot)]
        other_core = [(i, i ^ 1) for i in range(n_shard)]

        def gather(block):
            return lax.all_gather(block, "shard", axis=0, tiled=True)

        wholes, acc, grads = [], None, []
        if mode == "pair":
            early = lax.ppermute(blocks[2], "expert", partner)
            theirs = lax.ppermute(after(hidden, early), "expert", partner)
            last = None
            for chunk in range(col_chunks):
                block = blocks[chunk]
                if last is not None:
                    block = after(block, last)
                last = gather(block)
                wholes.append(last)
            early = gather(after(early, last))
            half = wholes[0].shape[0] // 2
            here, there = (lambda flag: flag[0]), (lambda flag: 1 - flag[0])
            for chunk in range(col_chunks):
                if chunk < col_chunks - 1:
                    send = lax.dynamic_slice_in_dim(wholes[chunk], core * half, half, axis=0)
                    got = lax.ppermute(send, "expert", partner)
                    rest = lax.ppermute(got, "shard", other_core)
                    parts = [(got, theirs, here), (rest, theirs, there)]
                    acc, grad = chunk_call(
                        chunk, flags, wholes[chunk], hidden, master, acc=acc, parts=parts
                    )
                    grads.append(grad)
                else:
                    parts = [(early, theirs, lambda flag: 0)]
                    return tuple(
                        chunk_call(
                            chunk, flags, wholes[chunk], hidden, master, acc=acc, parts=parts,
                            gate_up=gate_up, grads=grads,
                        )
                    )
        last = None
        for chunk in range(col_chunks):
            block = blocks[chunk]
            if last is not None:
                block = after(block, last)
            last = gather(block)
            wholes.append(last)
        if mode == "none":
            for chunk in range(col_chunks - 1):
                acc, grad = chunk_call(chunk, flags, wholes[chunk], hidden, master, acc=acc)
                grads.append(grad)
            return tuple(
                chunk_call(
                    col_chunks - 1, flags, last, hidden, master, acc=acc, gate_up=gate_up,
                    grads=grads,
                )
            )
        for chunk in range(col_chunks):
            final = chunk == col_chunks - 1
            outs = chunk_call(
                chunk, flags, wholes[chunk], hidden, master, acc=acc,
                gate_up=gate_up if final else None, grad_type=jnp.bfloat16,
            )
            grad = outs[-1]
            acc = outs[0]
            if mode == "four":
                groups = None
                if n_slot > 4:
                    groups = [list(range(i, i + 4)) for i in range(0, n_slot, 4)]
                if grads:
                    grad = after(grad, grads[-1])
                grad = lax.psum(grad, "expert", axis_index_groups=groups)
            else:
                for bit in (1, 2):
                    pairs = [(i, i ^ bit) for i in range(n_slot)]
                    got = lax.ppermute(grad, "expert", pairs)
                    grad = grad + jnp.where(share(bit), got, jnp.zeros((), got.dtype))
            grads.append(grad)
        return outs[0], outs[1], update_call(master, grads)

    modes = ["none", "pair", "four"] + (["mixed"] if n_slot > 4 else [])
    mixed = jnp.where(four_count == n_slot, 2, len(modes) - 1)
    which = jnp.where(four_count > 0, mixed, jnp.where(pair_count > 0, 1, 0))
    return lax.switch(
        which,
        [lambda *a, mode=mode: body(mode, *a) for mode in modes],
        grad_out, gate_pre, up_pre, counts, placement, master,
    )


def solution(mesh):
    return jax.shard_map(
        per_device,
        mesh=mesh,
        in_specs=(
            P("expert", "shard", None),
            P("expert", None, "shard"),
            P("expert", None, "shard"),
            P("expert", "shard"),
            P(),
            P("expert", "shard", None),
        ),
        out_specs=(
            P("expert", None, "shard"),
            P("expert", None, "shard"),
            P("expert", "shard", None),
        ),
        check_vma=False,
    )
```

```python
import functools

import jax
import jax.numpy as jnp
from jax import lax
from jax.experimental import pallas as pl
from jax.experimental.pallas import tpu as pltpu
from jax.sharding import PartitionSpec as P

learn_rate = 0.02
rms_eps = 1e-06
tall = 256
params = pltpu.CompilerParams(vmem_limit_bytes=48 * 2**20)


def dot(a, b, dims):
    return lax.dot_general(a, b, (dims, ((), ())), preferred_element_type=jnp.float32)


def hidden_kernel(gate_ref, up_ref, out_ref):
    gate = gate_ref[0].astype(jnp.float32)
    hidden = gate * jax.nn.sigmoid(gate) * up_ref[0].astype(jnp.float32)
    out_ref[...] = hidden.T.astype(out_ref.dtype)


def hidden_transposed(gate_pre, up_pre):
    _, rows, ffw = gate_pre.shape
    block = pl.BlockSpec((1, tall, ffw), lambda i: (0, i, 0))
    return pl.pallas_call(
        hidden_kernel,
        grid=(rows // tall,),
        in_specs=[block, block],
        out_specs=pl.BlockSpec((ffw, tall), lambda i: (0, i)),
        out_shape=jax.ShapeDtypeStruct((ffw, rows), jnp.bfloat16),
        compiler_params=params,
    )(gate_pre, up_pre)


def update_rows(master, grads, out_ref):
    square = sum(jnp.sum(g * g, axis=1, keepdims=True) for g in grads)
    scale = learn_rate / jnp.sqrt(square / master.shape[1] + rms_eps)
    first = 0
    for grad in grads:
        cols = slice(first, first + grad.shape[1])
        out_ref[0, :, cols] = master[:, cols] - grad * scale
        first += grad.shape[1]


def gates_back(d_hidden, gate_ref, up_ref, gate_out, up_out):
    gate = gate_ref[0].astype(jnp.float32)
    up = up_ref[0].astype(jnp.float32)
    sig = jax.nn.sigmoid(gate)
    up_out[0] = (d_hidden * (gate * sig)).astype(up_out.dtype)
    slope = sig * (1.0 + gate * (1.0 - sig))
    gate_out[0] = (d_hidden * up * slope).astype(gate_out.dtype)


def collect(flag_ref, pieces, layout, whole_ref, sem_ref):
    @pl.when(pl.program_id(0) == 0)
    def _():
        copies = []
        for place, (ref, index, row, first) in enumerate(layout):
            source = pieces[ref] if index is None else pieces[ref].at[index]
            high, wide = source.shape
            start = row if isinstance(row, int) else flag_ref[row[0]]
            start = pl.multiple_of(start, 128)
            target = whole_ref.at[pl.ds(start, high), pl.ds(first, wide)]
            copies.append(pltpu.make_async_copy(source, target, sem_ref.at[place]))
        for copy in copies:
            copy.start()
        for copy in copies:
            copy.wait()


def own_kernel(n_pieces, layout, update, flag_ref, *refs):
    pieces, refs = refs[:n_pieces], refs[n_pieces:]
    hidden_ref, master_ref, gate_ref, up_ref, gate_out, up_out, out_ref, whole_ref, sem_ref = refs
    collect(flag_ref, pieces, layout, whole_ref, sem_ref)
    grad = dot(hidden_ref[...], whole_ref[...], ((1,), (0,)))
    d_hidden = dot(whole_ref[...], master_ref[0].astype(jnp.bfloat16), ((1,), (1,)))
    gates_back(d_hidden, gate_ref, up_ref, gate_out, up_out)
    if update:
        update_rows(master_ref[0], [grad], out_ref)
    else:
        out_ref[...] = grad


def partner_kernel(n_pieces, layout, flag_ref, *refs):
    pieces, refs = refs[:n_pieces], refs[n_pieces:]
    hidden_ref, master_ref, grad_ref, out_ref, whole_ref, sem_ref = refs
    collect(flag_ref, pieces, layout, whole_ref, sem_ref)
    more = dot(hidden_ref[...], whole_ref[...], ((1,), (0,)))
    grad = grad_ref[...] + jnp.where(flag_ref[0] > 0, more, 0.0)
    update_rows(master_ref[0], [grad], out_ref)


def rows_call(flags, pieces, layout, hidden, master, gate_up=None, grad=None):
    ffw, rows = hidden.shape
    d_model = master.shape[2]
    full = pl.BlockSpec((1, tall, d_model), lambda i, flag: (0, i, 0))
    side = pl.BlockSpec((1, rows, tall), lambda i, flag: (0, 0, i))
    flat = pl.BlockSpec((tall, d_model), lambda i, flag: (i, 0))
    specs = [pl.BlockSpec(memory_space=pl.ANY)] * len(pieces)
    specs += [pl.BlockSpec((tall, rows), lambda i, flag: (i, 0)), full]
    args = [*pieces, hidden, master]
    new_master = jax.ShapeDtypeStruct(master.shape, master.dtype)
    if grad is not None:
        kernel = functools.partial(partner_kernel, len(pieces), layout)
        specs.append(flat)
        args.append(grad)
        out_specs, out_shape = full, new_master
    else:
        update = gate_up[2]
        kernel = functools.partial(own_kernel, len(pieces), layout, update)
        specs += [side, side]
        args += gate_up[:2]
        out_specs = [side, side, full if update else flat]
        out_shape = [jax.ShapeDtypeStruct(a.shape, a.dtype) for a in gate_up[:2]]
        out_shape.append(
            new_master if update else jax.ShapeDtypeStruct((ffw, d_model), jnp.float32)
        )
    return pl.pallas_call(
        kernel,
        grid_spec=pltpu.PrefetchScalarGridSpec(
            num_scalar_prefetch=1,
            grid=(ffw // tall,),
            in_specs=specs,
            out_specs=out_specs,
            scratch_shapes=[
                pltpu.VMEM((rows, d_model), jnp.bfloat16),
                pltpu.SemaphoreType.DMA((len(layout),)),
            ],
        ),
        out_shape=out_shape,
        compiler_params=params,
    )(flags, *args)


def chunk_kernel(has_acc, gates, own_ref, hidden_ref, master_ref, *refs):
    refs = list(refs)
    own = own_ref[...]
    grad = dot(hidden_ref[...], own, ((1,), (0,)))
    d_hidden = dot(own, master_ref[0].astype(jnp.bfloat16), ((1,), (1,)))
    if has_acc:
        d_hidden = d_hidden + refs.pop(0)[...]
    if gates:
        gate_ref, up_ref, gate_out, up_out, out_ref = refs
        gates_back(d_hidden, gate_ref, up_ref, gate_out, up_out)
    else:
        acc_out, out_ref = refs
        acc_out[...] = d_hidden
    out_ref[...] = grad.astype(out_ref.dtype)


def chunk_call(chunk, own, hidden, master, acc=None, gate_up=None):
    rows, width = own.shape
    ffw = hidden.shape[0]
    acc_spec = pl.BlockSpec((rows, tall), lambda i: (0, i))
    side = pl.BlockSpec((1, rows, tall), lambda i: (0, 0, i))
    specs = [
        pl.BlockSpec((rows, width), lambda i: (0, 0)),
        pl.BlockSpec((tall, rows), lambda i: (i, 0)),
        pl.BlockSpec((1, tall, width), lambda i: (0, i, chunk)),
    ]
    args = [own, hidden, master]
    if acc is not None:
        specs.append(acc_spec)
        args.append(acc)
    if gate_up is not None:
        specs += [side, side]
        args += list(gate_up)
        out_specs = [side, side]
        out_shape = [jax.ShapeDtypeStruct(a.shape, a.dtype) for a in gate_up]
    else:
        out_specs = [acc_spec]
        out_shape = [jax.ShapeDtypeStruct((rows, ffw), jnp.float32)]
    out_specs.append(pl.BlockSpec((tall, width), lambda i: (i, 0)))
    out_shape.append(jax.ShapeDtypeStruct((ffw, width), jnp.bfloat16))
    return pl.pallas_call(
        functools.partial(chunk_kernel, acc is not None, gate_up is not None),
        grid=(ffw // tall,),
        in_specs=specs,
        out_specs=out_specs,
        out_shape=out_shape,
        compiler_params=params,
    )(*args)


def update_kernel(master_ref, *refs):
    update_rows(master_ref[0], [r[...].astype(jnp.float32) for r in refs[:-1]], refs[-1])


def update_call(master, grads):
    _, ffw, d_model = master.shape
    full = pl.BlockSpec((1, 128, d_model), lambda i: (0, i, 0))
    part = pl.BlockSpec((128, grads[0].shape[1]), lambda i: (i, 0))
    return pl.pallas_call(
        update_kernel,
        grid=(ffw // 128,),
        in_specs=[full] + [part] * len(grads),
        out_specs=full,
        out_shape=jax.ShapeDtypeStruct(master.shape, master.dtype),
        compiler_params=params,
    )(master, *grads)


def after(value, other):
    return lax.optimization_barrier((value, other))[0]


def per_device(grad_out, gate_pre, up_pre, counts, placement, master):
    n_slot = lax.axis_size("expert")
    n_shard = lax.axis_size("shard")
    chips = n_shard // 2
    core = lax.axis_index("shard") % 2
    chip = lax.axis_index("shard") // 2
    slot = lax.axis_index("expert")
    rows, d_model = grad_out.shape[1:]
    order = jnp.arange(n_slot, dtype=jnp.int32)
    same = placement[:, None] == placement[None, :]
    pair_count = jnp.sum(same & (order[:, None] ^ 1 == order[None, :]), dtype=jnp.int32)
    four_count = jnp.sum(same & (order[:, None] ^ 2 == order[None, :]), dtype=jnp.int32)

    def share(bit):
        return jnp.any(same & (order[:, None] == slot) & (order[None, :] == slot ^ bit))

    def to_slot(value, bit):
        return lax.ppermute(value, "expert", [(i, i ^ bit) for i in range(n_slot)])

    def to_core(value):
        return lax.ppermute(value, "shard", [(i, i ^ 1) for i in range(n_shard)])

    def to_chip(value, pairs):
        pairs = [(2 * a + c, 2 * b + c) for a, b in pairs for c in range(2)]
        return lax.ppermute(value, "shard", pairs)

    def along_chips(block):
        if chips != 4:
            return [block] + [
                to_chip(block, [((z + far) % chips, z) for z in range(chips)])
                for far in range(1, chips)
            ]
        two = to_chip(block, [(0, 2), (1, 3), (2, 0), (3, 1)])
        one = to_chip(block, [(1, 0), (2, 1), (3, 2)])
        three = to_chip(block, [(0, 1), (1, 2), (2, 3)])
        end = to_chip(two, [(2, 3), (1, 0)])
        one = jnp.where(chip == 3, end, one)
        three = jnp.where(chip == 0, end, three)
        return [block, one, two, three]

    def all_sum(grad):
        half = grad.shape[0] // 2
        done = []
        for part, bits in ((grad[:half], (1, 2)), (grad[half:], (2, 1))):
            sides = [jnp.where(slot & bit > 0, 1, 0) for bit in bits]
            for bit, side in zip(bits, sides):
                high = part.shape[0] // 2
                keep = lax.dynamic_slice_in_dim(part, side * high, high)
                send = lax.dynamic_slice_in_dim(part, (1 - side) * high, high)
                got = to_slot(send, bit)
                part = (keep.astype(jnp.float32) + got.astype(jnp.float32)).astype(part.dtype)
            for bit, side in zip(bits[::-1], sides[::-1]):
                got = to_slot(part, bit)
                part = jnp.concatenate(
                    [jnp.where(side == 0, part, got), jnp.where(side == 0, got, part)]
                )
            done.append(part)
        return jnp.concatenate(done)

    def body(mode, grad_out, gate_pre, up_pre, counts, placement, master):
        live = jnp.arange(rows, dtype=jnp.int32) < counts[0, 0]
        masked = jnp.where(live[:, None], grad_out[0], jnp.zeros((), grad_out.dtype))

        def gather(block):
            return lax.all_gather(block, "shard", axis=0, tiled=True)

        if mode == "pair":
            middle = d_model * 2 // 3
            early = to_slot(masked[:, :middle], 1)
            mine = along_chips(masked)
            other = [to_core(piece) for piece in mine]
            hidden = hidden_transposed(gate_pre, up_pre)
            theirs = to_slot(hidden, 1)
            steps = [(chip + far) % chips for far in range(chips)]
            spots = [(2 * s + (core ^ swap)) * rows for swap in range(2) for s in steps]
            flags = jnp.stack([share(1).astype(jnp.int32)] + spots)
            layout = [(i, None, (1 + i,), 0) for i in range(n_shard)]
            late = to_slot(jnp.stack([piece[:, middle:] for piece in mine]), 1)
            first = along_chips(early)
            first = first + [to_core(piece) for piece in first]
            late = [late, to_core(late)]
            d_gate, d_up, grad = rows_call(
                flags, mine + other, layout, hidden, master, (gate_pre, up_pre, False)
            )
            layout = layout + [
                (n_shard + i // chips, i % chips, (1 + i,), middle) for i in range(n_shard)
            ]
            fresh = rows_call(flags, first + late, layout, theirs, master, grad=grad)
            return d_gate, d_up, fresh
        hidden = hidden_transposed(gate_pre, up_pre)
        if mode == "none":
            flags = jnp.zeros((1,), jnp.int32)
            layout = [(0, None, 0, 0)]
            return tuple(
                rows_call(
                    flags, [gather(masked)], layout, hidden, master, (gate_pre, up_pre, True)
                )
            )
        half = d_model // 2
        one = gather(masked[:, :half])
        two = gather(after(masked[:, half:], one))
        acc, grad_one = chunk_call(0, one, hidden, master)
        d_gate, d_up, grad_two = chunk_call(1, two, hidden, master, acc, (gate_pre, up_pre))
        grads = []
        for grad in (grad_one, grad_two):
            if mode == "four":
                grad = all_sum(grad)
            else:
                for bit in (1, 2):
                    got = to_slot(grad, bit)
                    grad = grad + jnp.where(share(bit), got, jnp.zeros((), got.dtype))
            grads.append(grad)
        return d_gate, d_up, update_call(master, grads)

    modes = ["none", "pair", "four"] + (["mixed"] if n_slot > 4 else [])
    mixed = jnp.where(four_count == n_slot, 2, len(modes) - 1)
    which = jnp.where(four_count > 0, mixed, jnp.where(pair_count > 0, 1, 0))
    return lax.switch(
        which,
        [lambda *a, mode=mode: body(mode, *a) for mode in modes],
        grad_out, gate_pre, up_pre, counts, placement, master,
    )


def solution(mesh):
    return jax.shard_map(
        per_device,
        mesh=mesh,
        in_specs=(
            P("expert", "shard", None),
            P("expert", None, "shard"),
            P("expert", None, "shard"),
            P("expert", "shard"),
            P(),
            P("expert", "shard", None),
        ),
        out_specs=(
            P("expert", None, "shard"),
            P("expert", None, "shard"),
            P("expert", "shard", None),
        ),
        check_vma=False,
    )
```

```python
import functools

import jax
import jax.numpy as jnp
from jax import lax
from jax.experimental import pallas as pl
from jax.experimental.pallas import tpu as pltpu
from jax.sharding import PartitionSpec as P

learn_rate = 0.02
rms_eps = 1e-06
tall = 256
params = pltpu.CompilerParams(vmem_limit_bytes=56 * 2**20)


def dot(a, b, dims):
    return lax.dot_general(a, b, (dims, ((), ())), preferred_element_type=jnp.float32)


def hidden_kernel(gate_ref, up_ref, out_ref):
    gate = gate_ref[0].astype(jnp.float32)
    hidden = gate * jax.nn.sigmoid(gate) * up_ref[0].astype(jnp.float32)
    out_ref[...] = hidden.T.astype(out_ref.dtype)


def hidden_transposed(gate_pre, up_pre):
    _, rows, ffw = gate_pre.shape
    block = pl.BlockSpec((1, tall, ffw), lambda i: (0, i, 0))
    return pl.pallas_call(
        hidden_kernel,
        grid=(rows // tall,),
        in_specs=[block, block],
        out_specs=pl.BlockSpec((ffw, tall), lambda i: (0, i)),
        out_shape=jax.ShapeDtypeStruct((ffw, rows), jnp.bfloat16),
        compiler_params=params,
    )(gate_pre, up_pre)


def update_rows(master, grads, out_ref):
    square = sum(jnp.sum(g * g, axis=1, keepdims=True) for g in grads)
    scale = learn_rate / jnp.sqrt(square / master.shape[1] + rms_eps)
    first = 0
    for grad in grads:
        cols = slice(first, first + grad.shape[1])
        out_ref[0, :, cols] = master[:, cols] - grad * scale
        first += grad.shape[1]


def gates_back(d_hidden, gate_ref, up_ref, gate_out, up_out):
    gate = gate_ref[0].astype(jnp.float32)
    up = up_ref[0].astype(jnp.float32)
    sig = jax.nn.sigmoid(gate)
    up_out[0] = (d_hidden * (gate * sig)).astype(up_out.dtype)
    slope = sig * (1.0 + gate * (1.0 - sig))
    gate_out[0] = (d_hidden * up * slope).astype(gate_out.dtype)


def phase_kernel(n_pieces, layout, wide, blocks, grad_in, gates, update, flag_ref, *refs):
    refs = list(refs)
    pieces = [refs.pop(0) for _ in range(n_pieces)]
    hidden_ref = refs.pop(0) if blocks else None
    master_hbm = refs.pop(0) if gates or update else None
    grad_ref = refs.pop(0) if grad_in else None
    gate_ref, up_ref = (refs.pop(0), refs.pop(0)) if gates else (None, None)
    gate_out, up_out = (refs.pop(0), refs.pop(0)) if gates else (None, None)
    out_ref = refs.pop(0) if blocks else None
    whole_ref, sem_ref = refs[:2]
    master_ref, master_sem = refs[2:4] if gates or update else (None, None)
    sum_ref = refs[4] if update else None
    step = pl.program_id(0)
    by_block = {}
    for place, (ref, index, row, source_first, first, count) in enumerate(layout):
        source = pieces[ref] if index is None else pieces[ref].at[index]
        high = source.shape[0]
        start = row if isinstance(row, int) else pl.multiple_of(flag_ref[row[0]], 128)
        copy = pltpu.make_async_copy(
            source.at[:, pl.ds(source_first, count)],
            whole_ref.at[pl.ds(start, high), pl.ds(first, count)],
            sem_ref.at[place],
        )
        by_block.setdefault(first // wide, []).append(copy)
    master_copies = []
    if gates or update:
        for i in range(master_ref.shape[0] // tall):
            lines = pl.ds(i * tall, tall)
            master_copies.append(
                pltpu.make_async_copy(
                    master_hbm.at[0, lines], master_ref.at[lines], master_sem.at[i]
                )
            )

    @pl.when(step == 0)
    def _():
        for block in sorted(by_block):
            for copy in by_block[block]:
                copy.start()
        for copy in master_copies:
            copy.start()

    for block in sorted(by_block):

        @pl.when(step == min(block, blocks))
        def _(block=block):
            for copy in by_block[block]:
                copy.wait()

    for i, copy in enumerate(master_copies):

        @pl.when(step == blocks + i)
        def _(copy=copy):
            copy.wait()

    if blocks:

        @pl.when(step < blocks)
        def _():
            cols = pl.ds(pl.multiple_of(step * wide, wide), wide)
            grad = dot(hidden_ref[...], whole_ref[:, cols], ((1,), (0,)))
            if grad_in:
                own = grad_ref[...].astype(jnp.float32)
                grad = own + jnp.where(flag_ref[0] > 0, grad, 0.0)
            if update:
                sum_ref[:, cols] = grad
            else:
                out_ref[...] = grad.astype(out_ref.dtype)

    if gates or update:

        @pl.when(step >= blocks)
        def _():
            lines = pl.ds(pl.multiple_of((step - blocks) * tall, tall), tall)
            if update:
                update_rows(master_ref[lines, :], [sum_ref[lines, :]], out_ref)
            if gates:
                weight = master_ref[lines, :].astype(jnp.bfloat16)
                d_hidden = dot(whole_ref[...], weight, ((1,), (1,)))
                gates_back(d_hidden, gate_ref, up_ref, gate_out, up_out)


def phase_call(flags, pieces, layout, hidden=None, master=None, grad=None, gate_up=None,
               update=False, d_model=None):
    if master is not None:
        _, ffw, d_model = master.shape
    else:
        ffw = hidden.shape[0]
    rows = gate_up[0].shape[1] if hidden is None else hidden.shape[1]
    wide = 512
    blocks = d_model // wide if hidden is not None else 0
    lines = ffw // tall if master is not None else 0
    cut = []
    for ref, index, row, first, count in layout:
        for at in range(0, count, wide):
            cut.append((ref, index, row, at, first + at, wide))
    row_block = lambda i: jnp.maximum(i - blocks, 0)
    col_block = lambda i: jnp.minimum(i, blocks - 1)
    anywhere = pl.BlockSpec(memory_space=pl.ANY)
    side = pl.BlockSpec((1, rows, tall), lambda i, flag: (0, 0, row_block(i)))
    full = pl.BlockSpec((1, tall, d_model), lambda i, flag: (0, row_block(i), 0))
    column = pl.BlockSpec((ffw, wide), lambda i, flag: (0, col_block(i)))
    specs, args = [anywhere] * len(pieces), list(pieces)
    out_specs, out_shape = [], []
    scratch = [
        pltpu.VMEM((rows, d_model), jnp.bfloat16),
        pltpu.SemaphoreType.DMA((len(cut),)),
    ]
    if hidden is not None:
        specs.append(pl.BlockSpec((ffw, rows), lambda i, flag: (0, 0)))
        args.append(hidden)
    if master is not None:
        specs.append(anywhere)
        args.append(master)
        scratch.append(pltpu.VMEM((ffw, d_model), jnp.float32))
        scratch.append(pltpu.SemaphoreType.DMA((lines,)))
    if grad is not None:
        specs.append(column)
        args.append(grad)
    if gate_up is not None:
        specs += [side, side]
        args += list(gate_up)
        out_specs += [side, side]
        out_shape += [jax.ShapeDtypeStruct(a.shape, a.dtype) for a in gate_up]
    if update:
        out_specs.append(full)
        out_shape.append(jax.ShapeDtypeStruct(master.shape, master.dtype))
        scratch.append(pltpu.VMEM((ffw, d_model), jnp.float32))
    elif hidden is not None:
        out_specs.append(column)
        out_shape.append(jax.ShapeDtypeStruct((ffw, d_model), jnp.bfloat16))
    dots = (hidden is not None) + (gate_up is not None)
    return pl.pallas_call(
        functools.partial(
            phase_kernel, len(pieces), cut, wide, blocks, grad is not None, gate_up is not None,
            update,
        ),
        grid_spec=pltpu.PrefetchScalarGridSpec(
            num_scalar_prefetch=1,
            grid=(blocks + lines,),
            in_specs=specs,
            out_specs=out_specs,
            scratch_shapes=scratch,
        ),
        out_shape=out_shape,
        compiler_params=params,
        cost_estimate=pl.CostEstimate(
            flops=2 * dots * rows * ffw * d_model,
            bytes_accessed=8 * ffw * d_model,
            transcendentals=0,
        ),
    )(flags, *args)


def update_kernel(master_ref, *refs):
    update_rows(master_ref[0], [r[...].astype(jnp.float32) for r in refs[:-1]], refs[-1])


def update_call(master, grads):
    _, ffw, d_model = master.shape
    full = pl.BlockSpec((1, 128, d_model), lambda i: (0, i, 0))
    part = pl.BlockSpec((128, grads[0].shape[1]), lambda i: (i, 0))
    return pl.pallas_call(
        update_kernel,
        grid=(ffw // 128,),
        in_specs=[full] + [part] * len(grads),
        out_specs=full,
        out_shape=jax.ShapeDtypeStruct(master.shape, master.dtype),
        compiler_params=params,
    )(master, *grads)


def after(value, other):
    return lax.optimization_barrier((value, other))[0]


def per_device(grad_out, gate_pre, up_pre, counts, placement, master):
    n_slot = lax.axis_size("expert")
    n_shard = lax.axis_size("shard")
    chips = n_shard // 2
    core = lax.axis_index("shard") % 2
    chip = lax.axis_index("shard") // 2
    slot = lax.axis_index("expert")
    rows, d_model = grad_out.shape[1:]
    order = jnp.arange(n_slot, dtype=jnp.int32)
    same = placement[:, None] == placement[None, :]
    pair_count = jnp.sum(same & (order[:, None] ^ 1 == order[None, :]), dtype=jnp.int32)
    four_count = jnp.sum(same & (order[:, None] ^ 2 == order[None, :]), dtype=jnp.int32)

    def share(bit):
        return jnp.any(same & (order[:, None] == slot) & (order[None, :] == slot ^ bit))

    def to_slot(value, bit):
        return lax.ppermute(value, "expert", [(i, i ^ bit) for i in range(n_slot)])

    def to_core(value):
        return lax.ppermute(value, "shard", [(i, i ^ 1) for i in range(n_shard)])

    def to_chip(value, pairs):
        pairs = [(2 * a + c, 2 * b + c) for a, b in pairs for c in range(2)]
        return lax.ppermute(value, "shard", pairs)

    def along_chips(block, held=None):
        if chips != 4:
            return [block] + [
                to_chip(block, [((z + far) % chips, z) for z in range(chips)])
                for far in range(1, chips)
            ]
        two = to_chip(block, [(0, 2), (1, 3), (2, 0), (3, 1)])
        one = to_chip(block, [(1, 0), (2, 1), (3, 2)])
        three = to_chip(block, [(0, 1), (1, 2), (2, 3)])
        end = to_chip(two if held is None else after(two, held), [(2, 3), (1, 0)])
        one = jnp.where(chip == 3, end, one)
        three = jnp.where(chip == 0, end, three)
        return [block, one, two, three]

    def all_sum(grad):
        half = grad.shape[0] // 2
        done = []
        for part, bits in ((grad[:half], (1, 2)), (grad[half:], (2, 1))):
            sides = [jnp.where(slot & bit > 0, 1, 0) for bit in bits]
            for bit, side in zip(bits, sides):
                high = part.shape[0] // 2
                keep = lax.dynamic_slice_in_dim(part, side * high, high)
                send = lax.dynamic_slice_in_dim(part, (1 - side) * high, high)
                got = to_slot(send, bit)
                part = (keep.astype(jnp.float32) + got.astype(jnp.float32)).astype(part.dtype)
            for bit, side in zip(bits[::-1], sides[::-1]):
                got = to_slot(part, bit)
                part = jnp.concatenate(
                    [jnp.where(side == 0, part, got), jnp.where(side == 0, got, part)]
                )
            done.append(part)
        return jnp.concatenate(done)

    def body(mode, grad_out, gate_pre, up_pre, counts, placement, master):
        live = jnp.arange(rows, dtype=jnp.int32) < counts[0, 0]
        masked = jnp.where(live[:, None], grad_out[0], jnp.zeros((), grad_out.dtype))

        def gather(block):
            return lax.all_gather(block, "shard", axis=0, tiled=True)

        gate_up = (gate_pre, up_pre)
        if mode == "pair":
            middle = d_model * 2 // 3
            early = to_slot(masked[:, :middle], 1)
            hidden = hidden_transposed(gate_pre, up_pre)
            high = hidden.shape[0] // 2
            top = to_slot(after(hidden[:high], early), 1)
            low = to_slot(after(hidden[high:], early), 1)
            mine = along_chips(masked, top)
            other = [to_core(piece) for piece in mine]
            first = along_chips(early)
            first = first + [to_core(piece) for piece in first]
            late = jnp.stack([piece[:, middle:] for piece in mine])
            late = to_slot(after(late, low), 1)
            late = [late, to_core(late)]
            theirs = jnp.concatenate([top, low])
            steps = [(chip + far) % chips for far in range(chips)]
            spots = [(2 * s + (core ^ swap)) * rows for swap in range(2) for s in steps]
            flags = jnp.stack([share(1).astype(jnp.int32)] + spots)
            layout = [(i, None, (1 + i,), 0, d_model) for i in range(n_shard)]
            d_gate, d_up, grad = phase_call(
                flags, after(mine, first[2]) + other, layout, hidden, master, gate_up=gate_up
            )
            layout = [(i, None, (1 + i,), 0, middle) for i in range(n_shard)]
            layout += [
                (n_shard + i // chips, i % chips, (1 + i,), middle, d_model - middle)
                for i in range(n_shard)
            ]
            fresh = phase_call(
                flags, first + late, layout, theirs, master, grad=grad, update=True
            )[0]
            return d_gate, d_up, fresh
        hidden = hidden_transposed(gate_pre, up_pre)
        flags = jnp.zeros((1,), jnp.int32)
        if mode == "none":
            layout = [(0, None, 0, 0, d_model)]
            return tuple(
                phase_call(
                    flags, [gather(masked)], layout, hidden, master, gate_up=gate_up, update=True
                )
            )
        half = d_model // 2
        one = gather(masked[:, :half])
        two = gather(after(masked[:, half:], one))
        layout = [(0, None, 0, 0, half)]
        grads = []
        for whole in (one, two):
            grad = phase_call(flags, [whole], layout, hidden, d_model=half)[0]
            if mode == "four":
                grad = all_sum(grad)
            else:
                for bit in (1, 2):
                    got = to_slot(grad, bit)
                    grad = grad + jnp.where(share(bit), got, jnp.zeros((), got.dtype))
            grads.append(grad)
        layout = layout + [(1, None, 0, half, half)]
        d_gate, d_up = phase_call(flags, [one, two], layout, master=master, gate_up=gate_up)
        return d_gate, d_up, update_call(master, grads)

    modes = ["none", "pair", "four"] + (["mixed"] if n_slot > 4 else [])
    mixed = jnp.where(four_count == n_slot, 2, len(modes) - 1)
    which = jnp.where(four_count > 0, mixed, jnp.where(pair_count > 0, 1, 0))
    return lax.switch(
        which,
        [lambda *a, mode=mode: body(mode, *a) for mode in modes],
        grad_out, gate_pre, up_pre, counts, placement, master,
    )


def solution(mesh):
    return jax.shard_map(
        per_device,
        mesh=mesh,
        in_specs=(
            P("expert", "shard", None),
            P("expert", None, "shard"),
            P("expert", None, "shard"),
            P("expert", "shard"),
            P(),
            P("expert", "shard", None),
        ),
        out_specs=(
            P("expert", None, "shard"),
            P("expert", None, "shard"),
            P("expert", "shard", None),
        ),
        check_vma=False,
    )
```

```python
import functools

import jax
import jax.numpy as jnp
from jax import lax
from jax.experimental import pallas as pl
from jax.experimental.pallas import tpu as pltpu
from jax.sharding import PartitionSpec as P

learn_rate = 0.02
rms_eps = 1e-06
tall = 256
params = pltpu.CompilerParams(vmem_limit_bytes=56 * 2**20)


def dot(a, b, dims):
    return lax.dot_general(a, b, (dims, ((), ())), preferred_element_type=jnp.float32)


def hidden_kernel(gate_ref, up_ref, out_ref):
    gate = gate_ref[0].astype(jnp.float32)
    hidden = gate * jax.nn.sigmoid(gate) * up_ref[0].astype(jnp.float32)
    out_ref[...] = hidden.T.astype(out_ref.dtype)


def hidden_transposed(gate_pre, up_pre):
    _, rows, ffw = gate_pre.shape
    block = pl.BlockSpec((1, tall, ffw), lambda i: (0, i, 0))
    return pl.pallas_call(
        hidden_kernel,
        grid=(rows // tall,),
        in_specs=[block, block],
        out_specs=pl.BlockSpec((ffw, tall), lambda i: (0, i)),
        out_shape=jax.ShapeDtypeStruct((ffw, rows), jnp.bfloat16),
        compiler_params=params,
    )(gate_pre, up_pre)


def update_rows(master, grads, out_ref):
    square = sum(jnp.sum(g * g, axis=1, keepdims=True) for g in grads)
    scale = learn_rate / jnp.sqrt(square / master.shape[1] + rms_eps)
    first = 0
    for grad in grads:
        cols = slice(first, first + grad.shape[1])
        out_ref[0, :, cols] = master[:, cols] - grad * scale
        first += grad.shape[1]


def gates_back(d_hidden, gate_ref, up_ref, gate_out, up_out):
    gate = gate_ref[0].astype(jnp.float32)
    up = up_ref[0].astype(jnp.float32)
    sig = jax.nn.sigmoid(gate)
    up_out[0] = (d_hidden * (gate * sig)).astype(up_out.dtype)
    slope = sig * (1.0 + gate * (1.0 - sig))
    gate_out[0] = (d_hidden * up * slope).astype(gate_out.dtype)


def phase_kernel(n_pieces, layout, wide, blocks, tall, grad_in, gates, update, flag_ref, *refs):
    refs = list(refs)
    pieces = [refs.pop(0) for _ in range(n_pieces)]
    hidden_ref = refs.pop(0) if blocks else None
    master_hbm = refs.pop(0) if gates or update else None
    grad_ref = refs.pop(0) if grad_in else None
    gate_ref, up_ref = (refs.pop(0), refs.pop(0)) if gates else (None, None)
    gate_out, up_out = (refs.pop(0), refs.pop(0)) if gates else (None, None)
    out_ref = refs.pop(0) if blocks else None
    whole_ref, sem_ref = refs[:2]
    master_ref, master_sem = refs[2:4] if gates or update else (None, None)
    sum_ref = refs[4] if update else None
    step = pl.program_id(0)
    by_block = {}
    for place, (ref, index, row, source_first, first, count) in enumerate(layout):
        source = pieces[ref] if index is None else pieces[ref].at[index]
        high = source.shape[0]
        start = row if isinstance(row, int) else pl.multiple_of(flag_ref[row[0]], 128)
        copy = pltpu.make_async_copy(
            source.at[:, pl.ds(source_first, count)],
            whole_ref.at[pl.ds(start, high), pl.ds(first, count)],
            sem_ref.at[place],
        )
        by_block.setdefault(first // wide, []).append(copy)
    master_copies = []
    if gates or update:
        for i in range(master_ref.shape[0] // tall):
            lines = pl.ds(i * tall, tall)
            master_copies.append(
                pltpu.make_async_copy(
                    master_hbm.at[0, lines], master_ref.at[lines], master_sem.at[i]
                )
            )

    @pl.when(step == 0)
    def _():
        for block in sorted(by_block):
            for copy in by_block[block]:
                copy.start()
        for copy in master_copies:
            copy.start()

    for block in sorted(by_block):

        @pl.when(step == min(block, blocks))
        def _(block=block):
            for copy in by_block[block]:
                copy.wait()

    for i, copy in enumerate(master_copies):

        @pl.when(step == blocks + i)
        def _(copy=copy):
            copy.wait()

    if blocks:

        @pl.when(step < blocks)
        def _():
            cols = pl.ds(pl.multiple_of(step * wide, wide), wide)
            grad = dot(hidden_ref[...], whole_ref[:, cols], ((1,), (0,)))
            if grad_in:
                own = grad_ref[...].astype(jnp.float32)
                grad = own + jnp.where(flag_ref[0] > 0, grad, 0.0)
            if update:
                sum_ref[:, cols] = grad
            else:
                out_ref[...] = grad.astype(out_ref.dtype)

    if gates or update:

        @pl.when(step >= blocks)
        def _():
            lines = pl.ds(pl.multiple_of((step - blocks) * tall, tall), tall)
            if update:
                update_rows(master_ref[lines, :], [sum_ref[lines, :]], out_ref)
            if gates:
                weight = master_ref[lines, :].astype(jnp.bfloat16)
                d_hidden = dot(whole_ref[...], weight, ((1,), (1,)))
                gates_back(d_hidden, gate_ref, up_ref, gate_out, up_out)


def phase_call(flags, pieces, layout, hidden=None, master=None, grad=None, gate_up=None,
               update=False, d_model=None, tall=256):
    if master is not None:
        _, ffw, d_model = master.shape
    else:
        ffw = hidden.shape[0]
    rows = gate_up[0].shape[1] if hidden is None else hidden.shape[1]
    wide = next(w for w in (1024, 768, 512, 128) if d_model % w == 0)
    blocks = d_model // wide if hidden is not None else 0
    lines = ffw // tall if master is not None else 0
    cut = []
    for ref, index, row, first, count in layout:
        piece = wide if blocks else count
        for at in range(0, count, piece):
            cut.append((ref, index, row, at, first + at, piece))
    row_block = lambda i: jnp.maximum(i - blocks, 0)
    col_block = lambda i: jnp.minimum(i, blocks - 1)
    anywhere = pl.BlockSpec(memory_space=pl.ANY)
    side = pl.BlockSpec((1, rows, tall), lambda i, flag: (0, 0, row_block(i)))
    full = pl.BlockSpec((1, tall, d_model), lambda i, flag: (0, row_block(i), 0))
    column = pl.BlockSpec((ffw, wide), lambda i, flag: (0, col_block(i)))
    specs, args = [anywhere] * len(pieces), list(pieces)
    out_specs, out_shape = [], []
    scratch = [
        pltpu.VMEM((rows, d_model), jnp.bfloat16),
        pltpu.SemaphoreType.DMA((len(cut),)),
    ]
    if hidden is not None:
        specs.append(pl.BlockSpec((ffw, rows), lambda i, flag: (0, 0), pipeline_mode=pl.Buffered(1)))
        args.append(hidden)
    if master is not None:
        specs.append(anywhere)
        args.append(master)
        scratch.append(pltpu.VMEM((ffw, d_model), jnp.float32))
        scratch.append(pltpu.SemaphoreType.DMA((lines,)))
    if grad is not None:
        specs.append(column)
        args.append(grad)
    if gate_up is not None:
        specs += [side, side]
        args += list(gate_up)
        out_specs += [side, side]
        out_shape += [jax.ShapeDtypeStruct(a.shape, a.dtype) for a in gate_up]
    if update:
        out_specs.append(full)
        out_shape.append(jax.ShapeDtypeStruct(master.shape, master.dtype))
        scratch.append(pltpu.VMEM((ffw, d_model), jnp.float32))
    elif hidden is not None:
        out_specs.append(column)
        out_shape.append(jax.ShapeDtypeStruct((ffw, d_model), jnp.bfloat16))
    dots = (hidden is not None) + (gate_up is not None)
    return pl.pallas_call(
        functools.partial(
            phase_kernel, len(pieces), cut, wide, blocks, tall, grad is not None, gate_up is not None,
            update,
        ),
        grid_spec=pltpu.PrefetchScalarGridSpec(
            num_scalar_prefetch=1,
            grid=(blocks + lines,),
            in_specs=specs,
            out_specs=out_specs,
            scratch_shapes=scratch,
        ),
        out_shape=out_shape,
        compiler_params=params,
        cost_estimate=pl.CostEstimate(
            flops=2 * dots * rows * ffw * d_model,
            bytes_accessed=8 * ffw * d_model,
            transcendentals=0,
        ),
    )(flags, *args)


def update_kernel(master_ref, *refs):
    update_rows(master_ref[0], [r[...].astype(jnp.float32) for r in refs[:-1]], refs[-1])


def update_call(master, grads):
    _, ffw, d_model = master.shape
    full = pl.BlockSpec((1, 128, d_model), lambda i: (0, i, 0))
    part = pl.BlockSpec((128, grads[0].shape[1]), lambda i: (i, 0))
    return pl.pallas_call(
        update_kernel,
        grid=(ffw // 128,),
        in_specs=[full] + [part] * len(grads),
        out_specs=full,
        out_shape=jax.ShapeDtypeStruct(master.shape, master.dtype),
        compiler_params=params,
    )(master, *grads)


def after(value, other):
    return lax.optimization_barrier((value, other))[0]


def per_device(grad_out, gate_pre, up_pre, counts, placement, master):
    n_slot = lax.axis_size("expert")
    n_shard = lax.axis_size("shard")
    chips = n_shard // 2
    core = lax.axis_index("shard") % 2
    chip = lax.axis_index("shard") // 2
    slot = lax.axis_index("expert")
    rows, d_model = grad_out.shape[1:]
    order = jnp.arange(n_slot, dtype=jnp.int32)
    same = placement[:, None] == placement[None, :]
    pair_count = jnp.sum(same & (order[:, None] ^ 1 == order[None, :]), dtype=jnp.int32)
    four_count = jnp.sum(same & (order[:, None] ^ 2 == order[None, :]), dtype=jnp.int32)

    def share(bit):
        return jnp.any(same & (order[:, None] == slot) & (order[None, :] == slot ^ bit))

    orders = {}

    def send(value, axis, pairs):
        turn = orders.get((axis, *sorted(pairs)), 0)
        orders[(axis, *sorted(pairs))] = turn + 1
        turn, back = divmod(turn, 2)
        pairs = pairs[turn:] + pairs[:turn]
        return lax.ppermute(value, axis, pairs[::-1] if back else pairs)

    def to_slot(value, bit):
        return send(value, "expert", [(i, i ^ bit) for i in range(n_slot)])

    def to_core(value):
        return send(value, "shard", [(i, i ^ 1) for i in range(n_shard)])

    def to_chip(value, pairs):
        return send(value, "shard", [(2 * a + c, 2 * b + c) for a, b in pairs for c in range(2)])

    def along_chips(block, held=None):
        if chips != 4:
            return [block] + [
                to_chip(block, [((z + far) % chips, z) for z in range(chips)])
                for far in range(1, chips)
            ]
        two = to_chip(block, [(0, 2), (1, 3), (2, 0), (3, 1)])
        one = to_chip(block, [(1, 0), (2, 1), (3, 2)])
        three = to_chip(block, [(0, 1), (1, 2), (2, 3)])
        end = to_chip(two if held is None else after(two, held), [(2, 3), (1, 0)])
        one = jnp.where(chip == 3, end, one)
        three = jnp.where(chip == 0, end, three)
        return [block, one, two, three]

    def all_sum(grad):
        half = grad.shape[0] // 2
        done = []
        for part, bits in ((grad[:half], (1, 2)), (grad[half:], (2, 1))):
            sides = [jnp.where(slot & bit > 0, 1, 0) for bit in bits]
            for bit, side in zip(bits, sides):
                high = part.shape[0] // 2
                keep = lax.dynamic_slice_in_dim(part, side * high, high)
                send = lax.dynamic_slice_in_dim(part, (1 - side) * high, high)
                got = to_slot(send, bit)
                part = (keep.astype(jnp.float32) + got.astype(jnp.float32)).astype(part.dtype)
            for bit, side in zip(bits[::-1], sides[::-1]):
                got = to_slot(part, bit)
                part = jnp.concatenate(
                    [jnp.where(side == 0, part, got), jnp.where(side == 0, got, part)]
                )
            done.append(part)
        return jnp.concatenate(done)

    def body(mode, grad_out, gate_pre, up_pre, counts, placement, master):
        orders.clear()
        live = jnp.arange(rows, dtype=jnp.int32) < counts[0, 0]
        masked = jnp.where(live[:, None], grad_out[0], jnp.zeros((), grad_out.dtype))

        def gather(block):
            return lax.all_gather(block, "shard", axis=0, tiled=True)

        gate_up = (gate_pre, up_pre)
        if mode == "pair":
            middle = d_model * 2 // 3
            early = to_slot(masked[:, :middle], 1)
            hidden = hidden_transposed(gate_pre, up_pre)
            high = hidden.shape[0] // 2
            top = to_slot(hidden[:high], 1)
            low = to_slot(hidden[high:], 1)
            mine = along_chips(masked, (early, top))
            other = [to_core(piece) for piece in mine]
            first = along_chips(early)
            late = to_slot(jnp.stack([piece[:, middle:] for piece in mine]), 1)
            theirs = jnp.concatenate([top, low])
            steps = [(chip + far) % chips for far in range(chips)]
            spots = [(2 * s + (core ^ swap)) * rows for swap in range(2) for s in steps]
            flags = jnp.stack([share(1).astype(jnp.int32)] + spots)
            layout = [(i, None, (1 + i,), 0, d_model) for i in range(n_shard)]
            d_gate, d_up, grad = phase_call(
                flags, after(mine, (first[2], low)) + other, layout, hidden, master,
                gate_up=gate_up, tall=512,
            )
            held = after(first[1:] + [late], grad)
            first = first + [to_core(piece) for piece in first[:1] + held[:-1]]
            late = [late, to_core(held[-1])]
            layout = [(i, None, (1 + i,), 0, middle) for i in range(n_shard)]
            layout += [
                (n_shard + i // chips, i % chips, (1 + i,), middle, d_model - middle)
                for i in range(n_shard)
            ]
            fresh = phase_call(
                flags, first + late, layout, theirs, master, grad=grad, update=True
            )[0]
            return d_gate, d_up, fresh
        hidden = hidden_transposed(gate_pre, up_pre)
        flags = jnp.zeros((1,), jnp.int32)
        if mode == "none":
            layout = [(0, None, 0, 0, d_model)]
            return tuple(
                phase_call(
                    flags, [gather(masked)], layout, hidden, master, gate_up=gate_up, update=True
                )
            )
        half = d_model // 2
        one = gather(masked[:, :half])
        two = gather(after(masked[:, half:], one))
        layout = [(0, None, 0, 0, half)]
        grads = []
        for whole in (one, two):
            grad = phase_call(flags, [whole], layout, hidden, d_model=half)[0]
            if mode == "four":
                grad = all_sum(grad)
            else:
                for bit in (1, 2):
                    got = to_slot(grad, bit)
                    grad = grad + jnp.where(share(bit), got, jnp.zeros((), got.dtype))
            grads.append(grad)
        layout = layout + [(1, None, 0, half, half)]
        d_gate, d_up = phase_call(flags, [one, two], layout, master=master, gate_up=gate_up, tall=512)
        return d_gate, d_up, update_call(master, grads)

    modes = ["none", "pair", "four"] + (["mixed"] if n_slot > 4 else [])
    mixed = jnp.where(four_count == n_slot, 2, len(modes) - 1)
    which = jnp.where(four_count > 0, mixed, jnp.where(pair_count > 0, 1, 0))
    return lax.switch(
        which,
        [lambda *a, mode=mode: body(mode, *a) for mode in modes],
        grad_out, gate_pre, up_pre, counts, placement, master,
    )


def solution(mesh):
    return jax.shard_map(
        per_device,
        mesh=mesh,
        in_specs=(
            P("expert", "shard", None),
            P("expert", None, "shard"),
            P("expert", None, "shard"),
            P("expert", "shard"),
            P(),
            P("expert", "shard", None),
        ),
        out_specs=(
            P("expert", None, "shard"),
            P("expert", None, "shard"),
            P("expert", "shard", None),
        ),
        check_vma=False,
    )
```

```python
import functools

import jax
import jax.numpy as jnp
from jax import lax
from jax.experimental import pallas as pl
from jax.experimental.pallas import tpu as pltpu
from jax.sharding import PartitionSpec as P

learn_rate = 0.02
rms_eps = 1e-06
tall = 256
params = pltpu.CompilerParams(vmem_limit_bytes=56 * 2**20)


def dot(a, b, dims):
    return lax.dot_general(a, b, (dims, ((), ())), preferred_element_type=jnp.float32)


def hidden_kernel(gate_ref, up_ref, out_ref):
    gate = gate_ref[0].astype(jnp.float32)
    hidden = gate * jax.nn.sigmoid(gate) * up_ref[0].astype(jnp.float32)
    out_ref[...] = hidden.T.astype(out_ref.dtype)


def hidden_transposed(gate_pre, up_pre):
    _, rows, ffw = gate_pre.shape
    block = pl.BlockSpec((1, tall, ffw), lambda i: (0, i, 0))
    return pl.pallas_call(
        hidden_kernel,
        grid=(rows // tall,),
        in_specs=[block, block],
        out_specs=pl.BlockSpec((ffw, tall), lambda i: (0, i)),
        out_shape=jax.ShapeDtypeStruct((ffw, rows), jnp.bfloat16),
        compiler_params=params,
    )(gate_pre, up_pre)


def update_rows(master, grads, out_ref):
    square = sum(jnp.sum(g * g, axis=1, keepdims=True) for g in grads)
    scale = learn_rate / jnp.sqrt(square / master.shape[1] + rms_eps)
    first = 0
    for grad in grads:
        cols = slice(first, first + grad.shape[1])
        out_ref[0, :, cols] = master[:, cols] - grad * scale
        first += grad.shape[1]


def gates_back(d_hidden, gate_ref, up_ref, gate_out, up_out):
    gate = gate_ref[0].astype(jnp.float32)
    up = up_ref[0].astype(jnp.float32)
    sig = jax.nn.sigmoid(gate)
    up_out[0] = (d_hidden * (gate * sig)).astype(up_out.dtype)
    slope = sig * (1.0 + gate * (1.0 - sig))
    gate_out[0] = (d_hidden * up * slope).astype(gate_out.dtype)


def phase_kernel(n_pieces, layout, wide, blocks, tall, grad_in, ready, gates, update, flag_ref,
                 *refs):
    refs = list(refs)
    pieces = [refs.pop(0) for _ in range(n_pieces)]
    hidden_ref = refs.pop(0) if blocks else None
    master_hbm = refs.pop(0) if gates or update else None
    grad_ref = refs.pop(0) if grad_in else None
    ready_ref = refs.pop(0) if ready else None
    gate_ref, up_ref = (refs.pop(0), refs.pop(0)) if gates else (None, None)
    gate_out, up_out = (refs.pop(0), refs.pop(0)) if gates else (None, None)
    out_ref = refs.pop(0) if blocks else None
    whole_ref, sem_ref = refs[:2]
    master_ref, master_sem = refs[2:4] if gates or update else (None, None)
    sum_ref = refs[4] if update else None
    step = pl.program_id(0)
    by_block = {}
    for place, (ref, index, row, source_first, first, count) in enumerate(layout):
        source = pieces[ref] if index is None else pieces[ref].at[index]
        high = source.shape[0]
        start = row if isinstance(row, int) else pl.multiple_of(flag_ref[row[0]], 128)
        copy = pltpu.make_async_copy(
            source.at[:, pl.ds(source_first, count)],
            whole_ref.at[pl.ds(start, high), pl.ds(first, count)],
            sem_ref.at[place],
        )
        by_block.setdefault(first // wide, []).append(copy)
    master_copies = []
    if gates or update:
        for i in range(master_ref.shape[0] // tall):
            lines = pl.ds(i * tall, tall)
            master_copies.append(
                pltpu.make_async_copy(
                    master_hbm.at[0, lines], master_ref.at[lines], master_sem.at[i]
                )
            )

    @pl.when(step == 0)
    def _():
        for block in sorted(by_block):
            for copy in by_block[block]:
                copy.start()
        for copy in master_copies:
            copy.start()

    for block in sorted(by_block):

        @pl.when(step == min(block, blocks))
        def _(block=block):
            for copy in by_block[block]:
                copy.wait()

    for i, copy in enumerate(master_copies):

        @pl.when(step == blocks + i)
        def _(copy=copy):
            copy.wait()

    if ready:

        @pl.when(step == 0)
        def _():
            sum_ref[:, :wide] = ready_ref[...].astype(jnp.float32)

    if blocks:

        @pl.when((step >= ready) & (step < blocks))
        def _():
            cols = pl.ds(pl.multiple_of(step * wide, wide), wide)
            grad = dot(hidden_ref[...], whole_ref[:, cols], ((1,), (0,)))
            if grad_in:
                own = grad_ref[...].astype(jnp.float32)
                grad = own + jnp.where(flag_ref[0] > 0, grad, 0.0)
            if update:
                sum_ref[:, cols] = grad
            else:
                out_ref[...] = grad.astype(out_ref.dtype)

    if gates or update:

        @pl.when(step >= blocks)
        def _():
            lines = pl.ds(pl.multiple_of((step - blocks) * tall, tall), tall)
            if update:
                update_rows(master_ref[lines, :], [sum_ref[lines, :]], out_ref)
            if gates:
                weight = master_ref[lines, :].astype(jnp.bfloat16)
                d_hidden = dot(whole_ref[...], weight, ((1,), (1,)))
                gates_back(d_hidden, gate_ref, up_ref, gate_out, up_out)


def phase_call(flags, pieces, layout, hidden=None, master=None, grad=None, gate_up=None,
               ready=None, update=False, d_model=None, tall=256):
    if master is not None:
        _, ffw, d_model = master.shape
    else:
        ffw = hidden.shape[0]
    rows = gate_up[0].shape[1] if hidden is None else hidden.shape[1]
    wide = next(w for w in (1024, 768, 512, 128) if d_model % w == 0)
    blocks = d_model // wide if hidden is not None else 0
    lines = ffw // tall if master is not None else 0
    cut = []
    for ref, index, row, first, count in layout:
        piece = wide if blocks else count
        for at in range(0, count, piece):
            cut.append((ref, index, row, at, first + at, piece))
    row_block = lambda i: jnp.maximum(i - blocks, 0)
    col_block = lambda i: jnp.minimum(i, blocks - 1)
    anywhere = pl.BlockSpec(memory_space=pl.ANY)
    side = pl.BlockSpec((1, rows, tall), lambda i, flag: (0, 0, row_block(i)))
    full = pl.BlockSpec((1, tall, d_model), lambda i, flag: (0, row_block(i), 0))
    column = pl.BlockSpec((ffw, wide), lambda i, flag: (0, col_block(i)))
    specs, args = [anywhere] * len(pieces), list(pieces)
    out_specs, out_shape = [], []
    scratch = [
        pltpu.VMEM((rows, d_model), jnp.bfloat16),
        pltpu.SemaphoreType.DMA((len(cut),)),
    ]
    if hidden is not None:
        specs.append(pl.BlockSpec((ffw, rows), lambda i, flag: (0, 0), pipeline_mode=pl.Buffered(1)))
        args.append(hidden)
    if master is not None:
        specs.append(anywhere)
        args.append(master)
        scratch.append(pltpu.VMEM((ffw, d_model), jnp.float32))
        scratch.append(pltpu.SemaphoreType.DMA((lines,)))
    if grad is not None:
        specs.append(column)
        args.append(grad)
    if ready is not None:
        specs.append(pl.BlockSpec((ffw, wide), lambda i, flag: (0, 0)))
        args.append(ready)
    if gate_up is not None:
        specs += [side, side]
        args += list(gate_up)
        out_specs += [side, side]
        out_shape += [jax.ShapeDtypeStruct(a.shape, a.dtype) for a in gate_up]
    if update:
        out_specs.append(full)
        out_shape.append(jax.ShapeDtypeStruct(master.shape, master.dtype))
        scratch.append(pltpu.VMEM((ffw, d_model), jnp.float32))
    elif hidden is not None:
        out_specs.append(column)
        out_shape.append(jax.ShapeDtypeStruct((ffw, d_model), jnp.bfloat16))
    dots = (hidden is not None) + (gate_up is not None)
    return pl.pallas_call(
        functools.partial(
            phase_kernel, len(pieces), cut, wide, blocks, tall, grad is not None,
            0 if ready is None else 1, gate_up is not None, update,
        ),
        grid_spec=pltpu.PrefetchScalarGridSpec(
            num_scalar_prefetch=1,
            grid=(blocks + lines,),
            in_specs=specs,
            out_specs=out_specs,
            scratch_shapes=scratch,
        ),
        out_shape=out_shape,
        compiler_params=params,
        cost_estimate=pl.CostEstimate(
            flops=2 * dots * rows * ffw * d_model,
            bytes_accessed=8 * ffw * d_model,
            transcendentals=0,
        ),
    )(flags, *args)


def update_kernel(master_ref, *refs):
    update_rows(master_ref[0], [r[...].astype(jnp.float32) for r in refs[:-1]], refs[-1])


def update_call(master, grads):
    _, ffw, d_model = master.shape
    full = pl.BlockSpec((1, 128, d_model), lambda i: (0, i, 0))
    part = pl.BlockSpec((128, grads[0].shape[1]), lambda i: (i, 0))
    return pl.pallas_call(
        update_kernel,
        grid=(ffw // 128,),
        in_specs=[full] + [part] * len(grads),
        out_specs=full,
        out_shape=jax.ShapeDtypeStruct(master.shape, master.dtype),
        compiler_params=params,
    )(master, *grads)


def after(value, other):
    return lax.optimization_barrier((value, other))[0]


def per_device(grad_out, gate_pre, up_pre, counts, placement, master):
    n_slot = lax.axis_size("expert")
    n_shard = lax.axis_size("shard")
    chips = n_shard // 2
    core = lax.axis_index("shard") % 2
    chip = lax.axis_index("shard") // 2
    slot = lax.axis_index("expert")
    rows, d_model = grad_out.shape[1:]
    order = jnp.arange(n_slot, dtype=jnp.int32)
    same = placement[:, None] == placement[None, :]
    pair_count = jnp.sum(same & (order[:, None] ^ 1 == order[None, :]), dtype=jnp.int32)
    four_count = jnp.sum(same & (order[:, None] ^ 2 == order[None, :]), dtype=jnp.int32)

    def share(bit):
        return jnp.any(same & (order[:, None] == slot) & (order[None, :] == slot ^ bit))

    orders = {}

    def send(value, axis, pairs):
        turn = orders.get((axis, *sorted(pairs)), 0)
        orders[(axis, *sorted(pairs))] = turn + 1
        turn, back = divmod(turn, 2)
        pairs = pairs[turn:] + pairs[:turn]
        return lax.ppermute(value, axis, pairs[::-1] if back else pairs)

    def to_slot(value, bit):
        return send(value, "expert", [(i, i ^ bit) for i in range(n_slot)])

    def to_core(value):
        return send(value, "shard", [(i, i ^ 1) for i in range(n_shard)])

    def to_chip(value, pairs):
        return send(value, "shard", [(2 * a + c, 2 * b + c) for a, b in pairs for c in range(2)])

    def along_chips(block, held=None):
        if chips != 4:
            return [block] + [
                to_chip(block, [((z + far) % chips, z) for z in range(chips)])
                for far in range(1, chips)
            ]
        two = to_chip(block, [(0, 2), (1, 3), (2, 0), (3, 1)])
        one = to_chip(block, [(1, 0), (2, 1), (3, 2)])
        three = to_chip(block, [(0, 1), (1, 2), (2, 3)])
        end = to_chip(two if held is None else after(two, held), [(2, 3), (1, 0)])
        one = jnp.where(chip == 3, end, one)
        three = jnp.where(chip == 0, end, three)
        return [block, one, two, three]

    def all_sum(grad):
        half = grad.shape[0] // 2
        done = []
        for part, bits in ((grad[:half], (1, 2)), (grad[half:], (2, 1))):
            sides = [jnp.where(slot & bit > 0, 1, 0) for bit in bits]
            for bit, side in zip(bits, sides):
                high = part.shape[0] // 2
                keep = lax.dynamic_slice_in_dim(part, side * high, high)
                send = lax.dynamic_slice_in_dim(part, (1 - side) * high, high)
                got = to_slot(send, bit)
                part = (keep.astype(jnp.float32) + got.astype(jnp.float32)).astype(part.dtype)
            for bit, side in zip(bits[::-1], sides[::-1]):
                got = to_slot(part, bit)
                part = jnp.concatenate(
                    [jnp.where(side == 0, part, got), jnp.where(side == 0, got, part)]
                )
            done.append(part)
        return jnp.concatenate(done)

    def body(mode, grad_out, gate_pre, up_pre, counts, placement, master):
        orders.clear()
        live = jnp.arange(rows, dtype=jnp.int32) < counts[0, 0]
        masked = jnp.where(live[:, None], grad_out[0], jnp.zeros((), grad_out.dtype))

        def gather(block):
            return lax.all_gather(block, "shard", axis=0, tiled=True)

        gate_up = (gate_pre, up_pre)
        if mode == "pair":
            width = d_model // 3
            middle = 2 * width
            early = to_slot(masked[:, :middle], 1)
            hidden = hidden_transposed(gate_pre, up_pre)
            high = hidden.shape[0] // 2
            top = to_slot(after(hidden[:high], early), 1)
            low = to_slot(hidden[high:], 1)
            mine = along_chips(masked, (early, top))
            other = [to_core(piece) for piece in mine]
            one = gather(early[:, :width])
            two = gather(after(early[:, width:], one))
            late = to_slot(jnp.stack([piece[:, middle:] for piece in mine]), 1)
            theirs = jnp.concatenate([top, low])
            steps = [(chip + far) % chips for far in range(chips)]
            spots = [(2 * s + (core ^ swap)) * rows for swap in range(2) for s in steps]
            flags = jnp.stack([share(1).astype(jnp.int32)] + spots)
            layout = [(i, None, (1 + i,), 0, d_model) for i in range(n_shard)]
            d_gate, d_up, grad = phase_call(
                flags, after(mine, (low, one)) + other, layout, hidden, master, gate_up=gate_up,
                tall=512,
            )
            ready = phase_call(
                flags, [one], [(0, None, 0, 0, width)], theirs, grad=grad, d_model=width
            )[0]
            rest = to_core(after(late, ready))
            layout = [(0, None, 0, width, width)] + [
                (1 + i // chips, i % chips, (1 + i,), middle, width) for i in range(n_shard)
            ]
            fresh = phase_call(
                flags, [two, late, rest], layout, theirs, master, grad=grad, ready=ready,
                update=True,
            )[0]
            return d_gate, d_up, fresh
        hidden = hidden_transposed(gate_pre, up_pre)
        flags = jnp.zeros((1,), jnp.int32)
        if mode == "none":
            layout = [(0, None, 0, 0, d_model)]
            return tuple(
                phase_call(
                    flags, [gather(masked)], layout, hidden, master, gate_up=gate_up, update=True
                )
            )
        half = d_model // 2
        one = gather(masked[:, :half])
        two = gather(after(masked[:, half:], one))
        layout = [(0, None, 0, 0, half)]
        grads = []
        for whole in (one, two):
            grad = phase_call(flags, [whole], layout, hidden, d_model=half)[0]
            if mode == "four":
                grad = all_sum(grad)
            else:
                for bit in (1, 2):
                    got = to_slot(grad, bit)
                    grad = grad + jnp.where(share(bit), got, jnp.zeros((), got.dtype))
            grads.append(grad)
        layout = layout + [(1, None, 0, half, half)]
        d_gate, d_up = phase_call(flags, [one, two], layout, master=master, gate_up=gate_up, tall=512)
        return d_gate, d_up, update_call(master, grads)

    modes = ["none", "pair", "four"] + (["mixed"] if n_slot > 4 else [])
    mixed = jnp.where(four_count == n_slot, 2, len(modes) - 1)
    which = jnp.where(four_count > 0, mixed, jnp.where(pair_count > 0, 1, 0))
    return lax.switch(
        which,
        [lambda *a, mode=mode: body(mode, *a) for mode in modes],
        grad_out, gate_pre, up_pre, counts, placement, master,
    )


def solution(mesh):
    return jax.shard_map(
        per_device,
        mesh=mesh,
        in_specs=(
            P("expert", "shard", None),
            P("expert", None, "shard"),
            P("expert", None, "shard"),
            P("expert", "shard"),
            P(),
            P("expert", "shard", None),
        ),
        out_specs=(
            P("expert", None, "shard"),
            P("expert", None, "shard"),
            P("expert", "shard", None),
        ),
        check_vma=False,
    )
```

```python
import functools

import jax
import jax.numpy as jnp
from jax import lax
from jax.experimental import pallas as pl
from jax.experimental.pallas import tpu as pltpu
from jax.sharding import PartitionSpec as P

learn_rate = 0.02
rms_eps = 1e-06
tall = 256
params = pltpu.CompilerParams(vmem_limit_bytes=56 * 2**20)


def dot(a, b, dims):
    return lax.dot_general(a, b, (dims, ((), ())), preferred_element_type=jnp.float32)


def hidden_kernel(gate_ref, up_ref, out_ref):
    gate = gate_ref[0].astype(jnp.float32)
    hidden = gate * jax.nn.sigmoid(gate) * up_ref[0].astype(jnp.float32)
    out_ref[...] = hidden.T.astype(out_ref.dtype)


def hidden_transposed(gate_pre, up_pre):
    _, rows, ffw = gate_pre.shape
    block = pl.BlockSpec((1, tall, ffw), lambda i: (0, i, 0))
    return pl.pallas_call(
        hidden_kernel,
        grid=(rows // tall,),
        in_specs=[block, block],
        out_specs=pl.BlockSpec((ffw, tall), lambda i: (0, i)),
        out_shape=jax.ShapeDtypeStruct((ffw, rows), jnp.bfloat16),
        compiler_params=params,
    )(gate_pre, up_pre)


def update_rows(master, grads, out_ref):
    square = sum(jnp.sum(g * g, axis=1, keepdims=True) for g in grads)
    scale = learn_rate / jnp.sqrt(square / master.shape[1] + rms_eps)
    first = 0
    for grad in grads:
        cols = slice(first, first + grad.shape[1])
        out_ref[0, :, cols] = master[:, cols] - grad * scale
        first += grad.shape[1]


def gates_back(d_hidden, gate_ref, up_ref, gate_out, up_out):
    gate = gate_ref[0].astype(jnp.float32)
    up = up_ref[0].astype(jnp.float32)
    sig = jax.nn.sigmoid(gate)
    up_out[0] = (d_hidden * (gate * sig)).astype(up_out.dtype)
    slope = sig * (1.0 + gate * (1.0 - sig))
    gate_out[0] = (d_hidden * up * slope).astype(gate_out.dtype)


def phase_kernel(n_pieces, layout, wide, blocks, tall, grad_in, ready, gates, update, flag_ref,
                 *refs):
    refs = list(refs)
    pieces = [refs.pop(0) for _ in range(n_pieces)]
    hidden_ref = refs.pop(0) if blocks else None
    master_hbm = refs.pop(0) if gates or update else None
    grad_ref = refs.pop(0) if grad_in else None
    ready_ref = refs.pop(0) if ready else None
    gate_ref, up_ref = (refs.pop(0), refs.pop(0)) if gates else (None, None)
    gate_out, up_out = (refs.pop(0), refs.pop(0)) if gates else (None, None)
    out_ref = refs.pop(0) if blocks else None
    whole_ref, sem_ref = refs[:2]
    master_ref, master_sem = refs[2:4] if gates or update else (None, None)
    sum_ref = refs[4] if update else None
    step = pl.program_id(0)
    by_block = {}
    for place, (ref, index, row, source_first, first, count) in enumerate(layout):
        source = pieces[ref] if index is None else pieces[ref].at[index]
        high = source.shape[0]
        start = row if isinstance(row, int) else pl.multiple_of(flag_ref[row[0]], 128)
        copy = pltpu.make_async_copy(
            source.at[:, pl.ds(source_first, count)],
            whole_ref.at[pl.ds(start, high), pl.ds(first, count)],
            sem_ref.at[place],
        )
        by_block.setdefault(first // wide, []).append(copy)
    master_copies = []
    if gates or update:
        for i in range(master_ref.shape[0] // tall):
            lines = pl.ds(i * tall, tall)
            master_copies.append(
                pltpu.make_async_copy(
                    master_hbm.at[0, lines], master_ref.at[lines], master_sem.at[i]
                )
            )

    @pl.when(step == 0)
    def _():
        for block in sorted(by_block):
            for copy in by_block[block]:
                copy.start()
        for copy in master_copies:
            copy.start()

    for block in sorted(by_block):

        @pl.when(step == min(block, blocks))
        def _(block=block):
            for copy in by_block[block]:
                copy.wait()

    for i, copy in enumerate(master_copies):

        @pl.when(step == blocks + i)
        def _(copy=copy):
            copy.wait()

    if ready:

        @pl.when(step == 0)
        def _():
            sum_ref[:, :wide] = ready_ref[...].astype(jnp.float32)

    if blocks:

        @pl.when((step >= ready) & (step < blocks))
        def _():
            cols = pl.ds(pl.multiple_of(step * wide, wide), wide)
            grad = dot(hidden_ref[...], whole_ref[:, cols], ((1,), (0,)))
            if grad_in:
                own = grad_ref[...].astype(jnp.float32)
                grad = own + jnp.where(flag_ref[0] > 0, grad, 0.0)
            if update:
                sum_ref[:, cols] = grad
            else:
                out_ref[...] = grad.astype(out_ref.dtype)

    if gates or update:

        @pl.when(step >= blocks)
        def _():
            lines = pl.ds(pl.multiple_of((step - blocks) * tall, tall), tall)
            if update:
                update_rows(master_ref[lines, :], [sum_ref[lines, :]], out_ref)
            if gates:
                weight = master_ref[lines, :].astype(jnp.bfloat16)
                d_hidden = dot(whole_ref[...], weight, ((1,), (1,)))
                gates_back(d_hidden, gate_ref, up_ref, gate_out, up_out)


def phase_call(flags, pieces, layout, hidden=None, master=None, grad=None, gate_up=None,
               ready=None, update=False, d_model=None, tall=256):
    if master is not None:
        _, ffw, d_model = master.shape
    else:
        ffw = hidden.shape[0]
    rows = gate_up[0].shape[1] if hidden is None else hidden.shape[1]
    wide = next(w for w in (1024, 768, 512, 128) if d_model % w == 0)
    blocks = d_model // wide if hidden is not None else 0
    lines = ffw // tall if master is not None else 0
    cut = []
    for ref, index, row, first, count in layout:
        piece = wide if blocks else count
        for at in range(0, count, piece):
            cut.append((ref, index, row, at, first + at, piece))
    row_block = lambda i: jnp.maximum(i - blocks, 0)
    col_block = lambda i: jnp.minimum(i, blocks - 1)
    anywhere = pl.BlockSpec(memory_space=pl.ANY)
    side = pl.BlockSpec((1, rows, tall), lambda i, flag: (0, 0, row_block(i)))
    full = pl.BlockSpec((1, tall, d_model), lambda i, flag: (0, row_block(i), 0))
    column = pl.BlockSpec((ffw, wide), lambda i, flag: (0, col_block(i)))
    specs, args = [anywhere] * len(pieces), list(pieces)
    out_specs, out_shape = [], []
    scratch = [
        pltpu.VMEM((rows, d_model), jnp.bfloat16),
        pltpu.SemaphoreType.DMA((len(cut),)),
    ]
    if hidden is not None:
        specs.append(pl.BlockSpec((ffw, rows), lambda i, flag: (0, 0), pipeline_mode=pl.Buffered(1)))
        args.append(hidden)
    if master is not None:
        specs.append(anywhere)
        args.append(master)
        scratch.append(pltpu.VMEM((ffw, d_model), jnp.float32))
        scratch.append(pltpu.SemaphoreType.DMA((lines,)))
    if grad is not None:
        specs.append(column)
        args.append(grad)
    if ready is not None:
        specs.append(pl.BlockSpec((ffw, wide), lambda i, flag: (0, 0)))
        args.append(ready)
    if gate_up is not None:
        specs += [side, side]
        args += list(gate_up)
        out_specs += [side, side]
        out_shape += [jax.ShapeDtypeStruct(a.shape, a.dtype) for a in gate_up]
    if update:
        out_specs.append(full)
        out_shape.append(jax.ShapeDtypeStruct(master.shape, master.dtype))
        scratch.append(pltpu.VMEM((ffw, d_model), jnp.float32))
    elif hidden is not None:
        out_specs.append(column)
        out_shape.append(jax.ShapeDtypeStruct((ffw, d_model), jnp.bfloat16))
    dots = (hidden is not None) + (gate_up is not None)
    return pl.pallas_call(
        functools.partial(
            phase_kernel, len(pieces), cut, wide, blocks, tall, grad is not None,
            0 if ready is None else 1, gate_up is not None, update,
        ),
        grid_spec=pltpu.PrefetchScalarGridSpec(
            num_scalar_prefetch=1,
            grid=(blocks + lines,),
            in_specs=specs,
            out_specs=out_specs,
            scratch_shapes=scratch,
        ),
        out_shape=out_shape,
        compiler_params=params,
        cost_estimate=pl.CostEstimate(
            flops=2 * dots * rows * ffw * d_model,
            bytes_accessed=8 * ffw * d_model,
            transcendentals=0,
        ),
    )(flags, *args)


def update_kernel(master_ref, *refs):
    update_rows(master_ref[0], [r[...].astype(jnp.float32) for r in refs[:-1]], refs[-1])


def update_call(master, grads):
    _, ffw, d_model = master.shape
    full = pl.BlockSpec((1, 128, d_model), lambda i: (0, i, 0))
    part = pl.BlockSpec((128, grads[0].shape[1]), lambda i: (i, 0))
    return pl.pallas_call(
        update_kernel,
        grid=(ffw // 128,),
        in_specs=[full] + [part] * len(grads),
        out_specs=full,
        out_shape=jax.ShapeDtypeStruct(master.shape, master.dtype),
        compiler_params=params,
    )(master, *grads)


def after(value, other):
    return lax.optimization_barrier((value, other))[0]


def per_device(grad_out, gate_pre, up_pre, counts, placement, master):
    n_slot = lax.axis_size("expert")
    n_shard = lax.axis_size("shard")
    chips = n_shard // 2
    core = lax.axis_index("shard") % 2
    chip = lax.axis_index("shard") // 2
    slot = lax.axis_index("expert")
    rows, d_model = grad_out.shape[1:]
    order = jnp.arange(n_slot, dtype=jnp.int32)
    same = placement[:, None] == placement[None, :]
    pair_count = jnp.sum(same & (order[:, None] ^ 1 == order[None, :]), dtype=jnp.int32)
    four_count = jnp.sum(same & (order[:, None] ^ 2 == order[None, :]), dtype=jnp.int32)

    def share(bit):
        return jnp.any(same & (order[:, None] == slot) & (order[None, :] == slot ^ bit))

    orders = {}

    def send(value, axis, pairs):
        turn = orders.get((axis, *sorted(pairs)), 0)
        orders[(axis, *sorted(pairs))] = turn + 1
        turn, back = divmod(turn, 2)
        pairs = pairs[turn:] + pairs[:turn]
        return lax.ppermute(value, axis, pairs[::-1] if back else pairs)

    def to_slot(value, bit):
        return send(value, "expert", [(i, i ^ bit) for i in range(n_slot)])

    def to_core(value):
        return send(value, "shard", [(i, i ^ 1) for i in range(n_shard)])

    def to_chip(value, pairs):
        return send(value, "shard", [(2 * a + c, 2 * b + c) for a, b in pairs for c in range(2)])

    def along_chips(block, held=None):
        if chips != 4:
            return [block] + [
                to_chip(block, [((z + far) % chips, z) for z in range(chips)])
                for far in range(1, chips)
            ]
        two = to_chip(block, [(0, 2), (1, 3), (2, 0), (3, 1)])
        one = to_chip(block, [(1, 0), (2, 1), (3, 2)])
        three = to_chip(block, [(0, 1), (1, 2), (2, 3)])
        end = to_chip(two if held is None else after(two, held), [(2, 3), (1, 0)])
        one = jnp.where(chip == 3, end, one)
        three = jnp.where(chip == 0, end, three)
        return [block, one, two, three]

    def all_sum(grad):
        half = grad.shape[0] // 2
        done = []
        for part, bits in ((grad[:half], (1, 2)), (grad[half:], (2, 1))):
            sides = [jnp.where(slot & bit > 0, 1, 0) for bit in bits]
            for bit, side in zip(bits, sides):
                high = part.shape[0] // 2
                keep = lax.dynamic_slice_in_dim(part, side * high, high)
                send = lax.dynamic_slice_in_dim(part, (1 - side) * high, high)
                got = to_slot(send, bit)
                part = (keep.astype(jnp.float32) + got.astype(jnp.float32)).astype(part.dtype)
            for bit, side in zip(bits[::-1], sides[::-1]):
                got = to_slot(part, bit)
                part = jnp.concatenate(
                    [jnp.where(side == 0, part, got), jnp.where(side == 0, got, part)]
                )
            done.append(part)
        return jnp.concatenate(done)

    def body(mode, grad_out, gate_pre, up_pre, counts, placement, master):
        orders.clear()
        live = jnp.arange(rows, dtype=jnp.int32) < counts[0, 0]
        masked = jnp.where(live[:, None], grad_out[0], jnp.zeros((), grad_out.dtype))

        def gather(block):
            return lax.all_gather(block, "shard", axis=0, tiled=True)

        gate_up = (gate_pre, up_pre)
        if mode == "pair":
            width = d_model // 3
            early = to_slot(masked[:, 2 * width :], 1)
            hidden = hidden_transposed(gate_pre, up_pre)
            theirs = to_slot(after(hidden, early), 1)
            one = gather(masked[:, :width])
            two = gather(after(masked[:, width:], one))
            last = gather(after(early, two))
            half = one.shape[0] // 2

            def to_partner(whole):
                return to_slot(lax.dynamic_slice(whole, (core * half, 0), (half, width)), 1)

            first = to_partner(one)
            second = to_partner(two)
            flags = jnp.stack([share(1).astype(jnp.int32), core * half, (1 - core) * half])
            layout = [(0, None, 0, 0, width), (1, None, 0, width, 2 * width)]
            d_gate, d_up, grad = phase_call(
                flags, after([one, two], theirs), layout, hidden, master, gate_up=gate_up,
                tall=512,
            )
            layout = [(0, None, (1,), 0, width), (1, None, (2,), 0, width)]
            ready = phase_call(
                flags, [first, to_core(first)], layout, theirs, grad=grad, d_model=width
            )[0]
            second = after(second, grad)
            layout = [
                (0, None, (1,), width, width),
                (1, None, (2,), width, width),
                (2, None, 0, 2 * width, width),
            ]
            fresh = phase_call(
                flags, [second, to_core(second), last], layout, theirs, master, grad=grad,
                ready=ready, update=True,
            )[0]
            return d_gate, d_up, fresh
        hidden = hidden_transposed(gate_pre, up_pre)
        flags = jnp.zeros((1,), jnp.int32)
        if mode == "none":
            layout = [(0, None, 0, 0, d_model)]
            return tuple(
                phase_call(
                    flags, [gather(masked)], layout, hidden, master, gate_up=gate_up, update=True
                )
            )
        half = d_model // 2
        one = gather(masked[:, :half])
        two = gather(after(masked[:, half:], one))
        layout = [(0, None, 0, 0, half)]
        grads = []
        for whole in (one, two):
            grad = phase_call(flags, [whole], layout, hidden, d_model=half)[0]
            if mode == "four":
                grad = all_sum(grad)
            else:
                for bit in (1, 2):
                    got = to_slot(grad, bit)
                    grad = grad + jnp.where(share(bit), got, jnp.zeros((), got.dtype))
            grads.append(grad)
        layout = layout + [(1, None, 0, half, half)]
        d_gate, d_up = phase_call(flags, [one, two], layout, master=master, gate_up=gate_up, tall=512)
        return d_gate, d_up, update_call(master, grads)

    modes = ["none", "pair", "four"] + (["mixed"] if n_slot > 4 else [])
    mixed = jnp.where(four_count == n_slot, 2, len(modes) - 1)
    which = jnp.where(four_count > 0, mixed, jnp.where(pair_count > 0, 1, 0))
    return lax.switch(
        which,
        [lambda *a, mode=mode: body(mode, *a) for mode in modes],
        grad_out, gate_pre, up_pre, counts, placement, master,
    )


def solution(mesh):
    return jax.shard_map(
        per_device,
        mesh=mesh,
        in_specs=(
            P("expert", "shard", None),
            P("expert", None, "shard"),
            P("expert", None, "shard"),
            P("expert", "shard"),
            P(),
            P("expert", "shard", None),
        ),
        out_specs=(
            P("expert", None, "shard"),
            P("expert", None, "shard"),
            P("expert", "shard", None),
        ),
        check_vma=False,
    )
```

```python
import functools

import jax
import jax.numpy as jnp
from jax import lax
from jax.experimental import pallas as pl
from jax.experimental.pallas import tpu as pltpu
from jax.sharding import PartitionSpec as P

learn_rate = 0.02
rms_eps = 1e-06
tall = 256
params = pltpu.CompilerParams(vmem_limit_bytes=56 * 2**20)


def dot(a, b, dims):
    return lax.dot_general(a, b, (dims, ((), ())), preferred_element_type=jnp.float32)


def hidden_kernel(gate_ref, up_ref, out_ref):
    gate = gate_ref[0].astype(jnp.float32)
    hidden = gate * jax.nn.sigmoid(gate) * up_ref[0].astype(jnp.float32)
    out_ref[...] = hidden.T.astype(out_ref.dtype)


def hidden_transposed(gate_pre, up_pre):
    _, rows, ffw = gate_pre.shape
    block = pl.BlockSpec((1, tall, ffw), lambda i: (0, i, 0))
    return pl.pallas_call(
        hidden_kernel,
        grid=(rows // tall,),
        in_specs=[block, block],
        out_specs=pl.BlockSpec((ffw, tall), lambda i: (0, i)),
        out_shape=jax.ShapeDtypeStruct((ffw, rows), jnp.bfloat16),
        compiler_params=params,
    )(gate_pre, up_pre)


def weight_kernel(master_ref, out_ref):
    out_ref[...] = master_ref[0].astype(out_ref.dtype).T


def weight_transposed(master):
    _, ffw, d_model = master.shape
    return pl.pallas_call(
        weight_kernel,
        grid=(ffw // tall,),
        in_specs=[pl.BlockSpec((1, tall, d_model), lambda i: (0, i, 0))],
        out_specs=pl.BlockSpec((d_model, tall), lambda i: (0, i)),
        out_shape=jax.ShapeDtypeStruct((d_model, ffw), jnp.bfloat16),
        compiler_params=params,
        cost_estimate=pl.CostEstimate(
            flops=0, bytes_accessed=6 * ffw * d_model, transcendentals=0
        ),
    )(master)


def update_rows(master, grads, out_ref):
    square = sum(jnp.sum(g * g, axis=1, keepdims=True) for g in grads)
    scale = learn_rate / jnp.sqrt(square / master.shape[1] + rms_eps)
    first = 0
    for grad in grads:
        cols = slice(first, first + grad.shape[1])
        out_ref[0, :, cols] = master[:, cols] - grad * scale
        first += grad.shape[1]


def gates_back(d_hidden, gate_ref, up_ref, gate_out, up_out):
    gate = gate_ref[0].astype(jnp.float32)
    up = up_ref[0].astype(jnp.float32)
    sig = jax.nn.sigmoid(gate)
    up_out[0] = (d_hidden * (gate * sig)).astype(up_out.dtype)
    slope = sig * (1.0 + gate * (1.0 - sig))
    gate_out[0] = (d_hidden * up * slope).astype(gate_out.dtype)


def phase_kernel(n_pieces, layout, wide, blocks, tall, grad_in, ready, gates, update, flag_ref,
                 *refs):
    refs = list(refs)
    pieces = [refs.pop(0) for _ in range(n_pieces)]
    hidden_ref = refs.pop(0) if blocks else None
    master_hbm = refs.pop(0) if update else None
    grad_ref = refs.pop(0) if grad_in else None
    ready_ref = refs.pop(0) if ready else None
    weight_ref, gate_ref, up_ref = [refs.pop(0) if gates else None for _ in range(3)]
    gate_out, up_out = (refs.pop(0), refs.pop(0)) if gates else (None, None)
    out_ref = refs.pop(0) if blocks else None
    whole_ref, sem_ref = refs[:2]
    master_ref, master_sem = refs[2:4] if update else (None, None)
    sum_ref = refs[4] if update else None
    step = pl.program_id(0)
    by_block = {}
    for place, (ref, index, row, source_first, first, count) in enumerate(layout):
        source = pieces[ref] if index is None else pieces[ref].at[index]
        high = source.shape[0]
        start = row if isinstance(row, int) else pl.multiple_of(flag_ref[row[0]], 128)
        copy = pltpu.make_async_copy(
            source.at[:, pl.ds(source_first, count)],
            whole_ref.at[pl.ds(start, high), pl.ds(first, count)],
            sem_ref.at[place],
        )
        by_block.setdefault(first // wide, []).append(copy)
    master_copies = []
    if update:
        for i in range(master_ref.shape[0] // tall):
            lines = pl.ds(i * tall, tall)
            master_copies.append(
                pltpu.make_async_copy(
                    master_hbm.at[0, lines], master_ref.at[lines], master_sem.at[i]
                )
            )

    @pl.when(step == 0)
    def _():
        for block in sorted(by_block):
            for copy in by_block[block]:
                copy.start()
        for copy in master_copies:
            copy.start()

    for block in sorted(by_block):

        @pl.when(step == min(block, blocks))
        def _(block=block):
            for copy in by_block[block]:
                copy.wait()

    for i, copy in enumerate(master_copies):

        @pl.when(step == blocks + i)
        def _(copy=copy):
            copy.wait()

    if ready:

        @pl.when(step == 0)
        def _():
            sum_ref[:, :wide] = ready_ref[...].astype(jnp.float32)

    if blocks:

        @pl.when((step >= ready) & (step < blocks))
        def _():
            cols = pl.ds(pl.multiple_of(step * wide, wide), wide)
            grad = dot(hidden_ref[...], whole_ref[:, cols], ((1,), (0,)))
            if grad_in:
                own = grad_ref[...].astype(jnp.float32)
                grad = own + jnp.where(flag_ref[0] > 0, grad, 0.0)
            if update:
                sum_ref[:, cols] = grad
            else:
                out_ref[...] = grad.astype(out_ref.dtype)

    if gates or update:

        @pl.when(step >= blocks)
        def _():
            lines = pl.ds(pl.multiple_of((step - blocks) * tall, tall), tall)
            if update:
                update_rows(master_ref[lines, :], [sum_ref[lines, :]], out_ref)
            if gates:
                d_hidden = dot(whole_ref[...], weight_ref[...], ((1,), (0,)))
                gates_back(d_hidden, gate_ref, up_ref, gate_out, up_out)


def phase_call(flags, pieces, layout, hidden=None, master=None, grad=None, gate_up=None,
               weight=None, ready=None, update=False, d_model=None):
    ffw = hidden.shape[0] if gate_up is None else gate_up[0].shape[2]
    if master is not None:
        d_model = master.shape[2]
    rows = gate_up[0].shape[1] if hidden is None else hidden.shape[1]
    wide = next(w for w in (1024, 768, 512, 128) if d_model % w == 0)
    blocks = d_model // wide if hidden is not None else 0
    lines = ffw // tall if update or gate_up is not None else 0
    cut = []
    for ref, index, row, first, count in layout:
        piece = wide if blocks else count
        for at in range(0, count, piece):
            cut.append((ref, index, row, at, first + at, piece))
    row_block = lambda i: jnp.maximum(i - blocks, 0)
    col_block = lambda i: jnp.minimum(i, blocks - 1)
    anywhere = pl.BlockSpec(memory_space=pl.ANY)
    side = pl.BlockSpec((1, rows, tall), lambda i, flag: (0, 0, row_block(i)))
    full = pl.BlockSpec((1, tall, d_model), lambda i, flag: (0, row_block(i), 0))
    column = pl.BlockSpec((ffw, wide), lambda i, flag: (0, col_block(i)))
    specs, args = [anywhere] * len(pieces), list(pieces)
    out_specs, out_shape = [], []
    scratch = [
        pltpu.VMEM((rows, d_model), jnp.bfloat16),
        pltpu.SemaphoreType.DMA((len(cut),)),
    ]
    if hidden is not None:
        specs.append(pl.BlockSpec((ffw, rows), lambda i, flag: (0, 0), pipeline_mode=pl.Buffered(1)))
        args.append(hidden)
    if master is not None:
        specs.append(anywhere)
        args.append(master)
        scratch.append(pltpu.VMEM((ffw, d_model), jnp.float32))
        scratch.append(pltpu.SemaphoreType.DMA((lines,)))
    if grad is not None:
        specs.append(column)
        args.append(grad)
    if ready is not None:
        specs.append(pl.BlockSpec((ffw, wide), lambda i, flag: (0, 0)))
        args.append(ready)
    if gate_up is not None:
        specs += [pl.BlockSpec((d_model, tall), lambda i, flag: (0, row_block(i))), side, side]
        args += [weight, *gate_up]
        out_specs += [side, side]
        out_shape += [jax.ShapeDtypeStruct(a.shape, a.dtype) for a in gate_up]
    if update:
        out_specs.append(full)
        out_shape.append(jax.ShapeDtypeStruct(master.shape, master.dtype))
        scratch.append(pltpu.VMEM((ffw, d_model), jnp.float32))
    elif hidden is not None:
        out_specs.append(column)
        out_shape.append(jax.ShapeDtypeStruct((ffw, d_model), jnp.bfloat16))
    dots = (hidden is not None) + (gate_up is not None)
    return pl.pallas_call(
        functools.partial(
            phase_kernel, len(pieces), cut, wide, blocks, tall, grad is not None,
            0 if ready is None else 1, gate_up is not None, update,
        ),
        grid_spec=pltpu.PrefetchScalarGridSpec(
            num_scalar_prefetch=1,
            grid=(blocks + lines,),
            in_specs=specs,
            out_specs=out_specs,
            scratch_shapes=scratch,
        ),
        out_shape=out_shape,
        compiler_params=params,
        cost_estimate=pl.CostEstimate(
            flops=2 * dots * rows * ffw * d_model,
            bytes_accessed=8 * ffw * d_model,
            transcendentals=0,
        ),
    )(flags, *args)


def update_kernel(master_ref, *refs):
    update_rows(master_ref[0], [r[...].astype(jnp.float32) for r in refs[:-1]], refs[-1])


def update_call(master, grads):
    _, ffw, d_model = master.shape
    full = pl.BlockSpec((1, 128, d_model), lambda i: (0, i, 0))
    part = pl.BlockSpec((128, grads[0].shape[1]), lambda i: (i, 0))
    return pl.pallas_call(
        update_kernel,
        grid=(ffw // 128,),
        in_specs=[full] + [part] * len(grads),
        out_specs=full,
        out_shape=jax.ShapeDtypeStruct(master.shape, master.dtype),
        compiler_params=pltpu.CompilerParams(vmem_limit_bytes=20 * 2**20),
    )(master, *grads)


def after(value, other):
    return lax.optimization_barrier((value, other))[0]


def per_device(grad_out, gate_pre, up_pre, counts, placement, master):
    n_slot = lax.axis_size("expert")
    n_shard = lax.axis_size("shard")
    chips = n_shard // 2
    core = lax.axis_index("shard") % 2
    chip = lax.axis_index("shard") // 2
    slot = lax.axis_index("expert")
    rows, d_model = grad_out.shape[1:]
    order = jnp.arange(n_slot, dtype=jnp.int32)
    same = placement[:, None] == placement[None, :]
    pair_count = jnp.sum(same & (order[:, None] ^ 1 == order[None, :]), dtype=jnp.int32)
    four_count = jnp.sum(same & (order[:, None] ^ 2 == order[None, :]), dtype=jnp.int32)

    def share(bit):
        return jnp.any(same & (order[:, None] == slot) & (order[None, :] == slot ^ bit))

    orders = {}

    def send(value, axis, pairs):
        turn = orders.get((axis, *sorted(pairs)), 0)
        orders[(axis, *sorted(pairs))] = turn + 1
        turn, back = divmod(turn, 2)
        pairs = pairs[turn:] + pairs[:turn]
        return lax.ppermute(value, axis, pairs[::-1] if back else pairs)

    def to_slot(value, bit):
        return send(value, "expert", [(i, i ^ bit) for i in range(n_slot)])

    def to_core(value):
        return send(value, "shard", [(i, i ^ 1) for i in range(n_shard)])

    def to_chip(value, pairs):
        return send(value, "shard", [(2 * a + c, 2 * b + c) for a, b in pairs for c in range(2)])

    def along_chips(block, held=None):
        if chips != 4:
            return [block] + [
                to_chip(block, [((z + far) % chips, z) for z in range(chips)])
                for far in range(1, chips)
            ]
        two = to_chip(block, [(0, 2), (1, 3), (2, 0), (3, 1)])
        one = to_chip(block, [(1, 0), (2, 1), (3, 2)])
        three = to_chip(block, [(0, 1), (1, 2), (2, 3)])
        end = to_chip(two if held is None else after(two, held), [(2, 3), (1, 0)])
        one = jnp.where(chip == 3, end, one)
        three = jnp.where(chip == 0, end, three)
        return [block, one, two, three]

    def all_sum(grad, held):
        half = grad.shape[0] // 2
        done = []
        for part, bits in ((grad[:half], (1, 2)), (grad[half:], (2, 1))):
            sides = [jnp.where(slot & bit > 0, 1, 0) for bit in bits]
            for bit, side in zip(bits, sides):
                high = part.shape[0] // 2
                keep = lax.dynamic_slice_in_dim(part, side * high, high)
                send = lax.dynamic_slice_in_dim(part, (1 - side) * high, high)
                got = to_slot(send, bit)
                part = (keep.astype(jnp.float32) + got.astype(jnp.float32)).astype(part.dtype)
            part = after(part, held)
            for bit, side in zip(bits[::-1], sides[::-1]):
                got = to_slot(part, bit)
                part = jnp.concatenate(
                    [jnp.where(side == 0, part, got), jnp.where(side == 0, got, part)]
                )
            done.append(part)
        return jnp.concatenate(done)

    def body(mode, grad_out, gate_pre, up_pre, counts, placement, master):
        orders.clear()
        live = jnp.arange(rows, dtype=jnp.int32) < counts[0, 0]
        masked = jnp.where(live[:, None], grad_out[0], jnp.zeros((), grad_out.dtype))

        def gather(block):
            return lax.all_gather(block, "shard", axis=0, tiled=True)

        gate_up = (gate_pre, up_pre)
        if mode == "pair":
            width = d_model // 3
            early = to_slot(masked[:, 2 * width :], 1)
            hidden = hidden_transposed(gate_pre, up_pre)
            theirs = to_slot(after(hidden, early), 1)
            one = gather(masked[:, :width])
            two = gather(after(masked[:, width:], one))
            last = gather(after(early, two))
            half = one.shape[0] // 2

            def to_partner(whole):
                return to_slot(lax.dynamic_slice(whole, (core * half, 0), (half, width)), 1)

            weight = weight_transposed(master)
            first = to_partner(after(one, weight))
            second = to_partner(two)
            flags = jnp.stack([share(1).astype(jnp.int32), core * half, (1 - core) * half])
            layout = [(0, None, 0, 0, width), (1, None, 0, width, 2 * width)]
            d_gate, d_up, grad = phase_call(
                flags, after([one, two], theirs), layout, hidden, gate_up=gate_up, weight=weight,
                d_model=d_model,
            )
            layout = [(0, None, (1,), 0, width), (1, None, (2,), 0, width)]
            ready = phase_call(
                flags, [first, to_core(first)], layout, theirs, grad=grad, d_model=width
            )[0]
            second = after(second, grad)
            layout = [
                (0, None, (1,), width, width),
                (1, None, (2,), width, width),
                (2, None, 0, 2 * width, width),
            ]
            fresh = phase_call(
                flags, [second, to_core(second), last], layout, theirs, master, grad=grad,
                ready=ready, update=True,
            )[0]
            return d_gate, d_up, fresh
        hidden = hidden_transposed(gate_pre, up_pre)
        weight = weight_transposed(master)
        flags = jnp.zeros((1,), jnp.int32)
        if mode == "none":
            layout = [(0, None, 0, 0, d_model)]
            return tuple(
                phase_call(
                    flags, [gather(masked)], layout, hidden, master, gate_up=gate_up,
                    weight=weight, update=True,
                )
            )
        width = d_model // 3
        wholes, grads = [], []
        for first in range(0, d_model, width):
            block = masked[:, first : first + width]
            wholes.append(gather(after(block, wholes[-1]) if wholes else block))
            layout = [(0, None, 0, 0, width)]
            grads.append(phase_call(flags, wholes[-1:], layout, hidden, d_model=width)[0])
        layout = [(i, None, 0, i * width, width) for i in range(3)]
        d_gate, d_up = phase_call(
            flags, wholes, layout, gate_up=gate_up, weight=weight, d_model=d_model
        )
        held = grads[1:] + [d_gate]
        for i, grad in enumerate(grads):
            if mode == "four":
                grads[i] = all_sum(grad, held[i])
                continue
            for bit in (1, 2):
                got = to_slot(grads[i], bit)
                grads[i] = grads[i] + jnp.where(share(bit), got, jnp.zeros((), got.dtype))
        return d_gate, d_up, update_call(master, grads)

    modes = ["none", "pair", "four"] + (["mixed"] if n_slot > 4 else [])
    mixed = jnp.where(four_count == n_slot, 2, len(modes) - 1)
    which = jnp.where(four_count > 0, mixed, jnp.where(pair_count > 0, 1, 0))
    return lax.switch(
        which,
        [lambda *a, mode=mode: body(mode, *a) for mode in modes],
        grad_out, gate_pre, up_pre, counts, placement, master,
    )


def solution(mesh):
    return jax.shard_map(
        per_device,
        mesh=mesh,
        in_specs=(
            P("expert", "shard", None),
            P("expert", None, "shard"),
            P("expert", None, "shard"),
            P("expert", "shard"),
            P(),
            P("expert", "shard", None),
        ),
        out_specs=(
            P("expert", None, "shard"),
            P("expert", None, "shard"),
            P("expert", "shard", None),
        ),
        check_vma=False,
    )
```

```python
import functools

import jax
import jax.numpy as jnp
from jax import lax
from jax.experimental import pallas as pl
from jax.experimental.pallas import tpu as pltpu
from jax.sharding import PartitionSpec as P

learn_rate = 0.02
rms_eps = 1e-06
tall = 256
params = pltpu.CompilerParams(vmem_limit_bytes=56 * 2**20)


def dot(a, b, dims):
    return lax.dot_general(a, b, (dims, ((), ())), preferred_element_type=jnp.float32)


def hidden_kernel(gate_ref, up_ref, out_ref):
    gate = gate_ref[0].astype(jnp.float32)
    hidden = gate * jax.nn.sigmoid(gate) * up_ref[0].astype(jnp.float32)
    out_ref[...] = hidden.T.astype(out_ref.dtype)


def hidden_transposed(gate_pre, up_pre):
    _, rows, ffw = gate_pre.shape
    block = pl.BlockSpec((1, tall, ffw), lambda i: (0, i, 0))
    return pl.pallas_call(
        hidden_kernel,
        grid=(rows // tall,),
        in_specs=[block, block],
        out_specs=pl.BlockSpec((ffw, tall), lambda i: (0, i)),
        out_shape=jax.ShapeDtypeStruct((ffw, rows), jnp.bfloat16),
        compiler_params=params,
    )(gate_pre, up_pre)


def weight_kernel(master_ref, out_ref):
    out_ref[...] = master_ref[0].astype(out_ref.dtype).T


def weight_transposed(master):
    _, ffw, d_model = master.shape
    return pl.pallas_call(
        weight_kernel,
        grid=(ffw // tall,),
        in_specs=[pl.BlockSpec((1, tall, d_model), lambda i: (0, i, 0))],
        out_specs=pl.BlockSpec((d_model, tall), lambda i: (0, i)),
        out_shape=jax.ShapeDtypeStruct((d_model, ffw), jnp.bfloat16),
        compiler_params=params,
        cost_estimate=pl.CostEstimate(
            flops=0, bytes_accessed=6 * ffw * d_model, transcendentals=0
        ),
    )(master)


def update_rows(master, grads, out_ref):
    square = sum(jnp.sum(g * g, axis=1, keepdims=True) for g in grads)
    scale = learn_rate / jnp.sqrt(square / master.shape[1] + rms_eps)
    first = 0
    for grad in grads:
        cols = slice(first, first + grad.shape[1])
        out_ref[0, :, cols] = master[:, cols] - grad * scale
        first += grad.shape[1]


def gates_back(d_hidden, gate_ref, up_ref, gate_out, up_out):
    gate = gate_ref[0].astype(jnp.float32)
    up = up_ref[0].astype(jnp.float32)
    sig = jax.nn.sigmoid(gate)
    up_out[0] = (d_hidden * (gate * sig)).astype(up_out.dtype)
    slope = sig * (1.0 + gate * (1.0 - sig))
    gate_out[0] = (d_hidden * up * slope).astype(gate_out.dtype)


def phase_kernel(n_pieces, layout, wide, blocks, tall, grad_in, ready, gates, update, flag_ref,
                 *refs):
    refs = list(refs)
    pieces = [refs.pop(0) for _ in range(n_pieces)]
    hidden_ref = refs.pop(0) if blocks else None
    master_hbm = refs.pop(0) if update else None
    grad_ref = refs.pop(0) if grad_in else None
    ready_ref = refs.pop(0) if ready else None
    weight_ref, gate_ref, up_ref = [refs.pop(0) if gates else None for _ in range(3)]
    gate_out, up_out = (refs.pop(0), refs.pop(0)) if gates else (None, None)
    out_ref = refs.pop(0) if blocks else None
    whole_ref, sem_ref = refs[:2]
    master_ref, master_sem = refs[2:4] if update else (None, None)
    sum_ref = refs[4] if update else None
    step = pl.program_id(0)
    by_block = {}
    for place, (ref, index, row, source_first, first, count) in enumerate(layout):
        source = pieces[ref] if index is None else pieces[ref].at[index]
        high = source.shape[0]
        start = row if isinstance(row, int) else pl.multiple_of(flag_ref[row[0]], 128)
        copy = pltpu.make_async_copy(
            source.at[:, pl.ds(source_first, count)],
            whole_ref.at[pl.ds(start, high), pl.ds(first, count)],
            sem_ref.at[place],
        )
        by_block.setdefault(first // wide, []).append(copy)
    master_copies = []
    if update:
        for i in range(master_ref.shape[0] // tall):
            lines = pl.ds(i * tall, tall)
            master_copies.append(
                pltpu.make_async_copy(
                    master_hbm.at[0, lines], master_ref.at[lines], master_sem.at[i]
                )
            )

    @pl.when(step == 0)
    def _():
        for block in sorted(by_block):
            for copy in by_block[block]:
                copy.start()
        for copy in master_copies:
            copy.start()

    for block in sorted(by_block):

        @pl.when(step == min(block, blocks))
        def _(block=block):
            for copy in by_block[block]:
                copy.wait()

    for i, copy in enumerate(master_copies):

        @pl.when(step == blocks + i)
        def _(copy=copy):
            copy.wait()

    if ready:

        @pl.when(step == 0)
        def _():
            sum_ref[:, :wide] = ready_ref[...].astype(jnp.float32)

    if blocks:

        @pl.when((step >= ready) & (step < blocks))
        def _():
            cols = pl.ds(pl.multiple_of(step * wide, wide), wide)
            grad = dot(hidden_ref[...], whole_ref[:, cols], ((1,), (0,)))
            if grad_in:
                own = grad_ref[...].astype(jnp.float32)
                grad = own + jnp.where(flag_ref[0] > 0, grad, 0.0)
            if update:
                sum_ref[:, cols] = grad
            else:
                out_ref[...] = grad.astype(out_ref.dtype)

    if gates or update:

        @pl.when(step >= blocks)
        def _():
            lines = pl.ds(pl.multiple_of((step - blocks) * tall, tall), tall)
            if update:
                update_rows(master_ref[lines, :], [sum_ref[lines, :]], out_ref)
            if gates:
                d_hidden = dot(whole_ref[...], weight_ref[...], ((1,), (0,)))
                gates_back(d_hidden, gate_ref, up_ref, gate_out, up_out)


def phase_call(flags, pieces, layout, hidden=None, master=None, grad=None, gate_up=None,
               weight=None, ready=None, update=False, d_model=None):
    ffw = hidden.shape[0] if gate_up is None else gate_up[0].shape[2]
    if master is not None:
        d_model = master.shape[2]
    rows = gate_up[0].shape[1] if hidden is None else hidden.shape[1]
    wide = next(w for w in (1024, 768, 512, 128) if d_model % w == 0)
    blocks = d_model // wide if hidden is not None else 0
    lines = ffw // tall if update or gate_up is not None else 0
    cut = []
    for ref, index, row, first, count in layout:
        piece = wide if blocks else count
        for at in range(0, count, piece):
            cut.append((ref, index, row, at, first + at, piece))
    row_block = lambda i: jnp.maximum(i - blocks, 0)
    col_block = lambda i: jnp.minimum(i, blocks - 1)
    anywhere = pl.BlockSpec(memory_space=pl.ANY)
    side = pl.BlockSpec((1, rows, tall), lambda i, flag: (0, 0, row_block(i)))
    full = pl.BlockSpec((1, tall, d_model), lambda i, flag: (0, row_block(i), 0))
    column = pl.BlockSpec((ffw, wide), lambda i, flag: (0, col_block(i)))
    specs, args = [anywhere] * len(pieces), list(pieces)
    out_specs, out_shape = [], []
    scratch = [
        pltpu.VMEM((rows, d_model), jnp.bfloat16),
        pltpu.SemaphoreType.DMA((len(cut),)),
    ]
    if hidden is not None:
        specs.append(pl.BlockSpec((ffw, rows), lambda i, flag: (0, 0), pipeline_mode=pl.Buffered(1)))
        args.append(hidden)
    if master is not None:
        specs.append(anywhere)
        args.append(master)
        scratch.append(pltpu.VMEM((ffw, d_model), jnp.float32))
        scratch.append(pltpu.SemaphoreType.DMA((lines,)))
    if grad is not None:
        specs.append(column)
        args.append(grad)
    if ready is not None:
        specs.append(pl.BlockSpec((ffw, wide), lambda i, flag: (0, 0)))
        args.append(ready)
    if gate_up is not None:
        specs += [pl.BlockSpec((d_model, tall), lambda i, flag: (0, row_block(i))), side, side]
        args += [weight, *gate_up]
        out_specs += [side, side]
        out_shape += [jax.ShapeDtypeStruct(a.shape, a.dtype) for a in gate_up]
    if update:
        out_specs.append(full)
        out_shape.append(jax.ShapeDtypeStruct(master.shape, master.dtype))
        scratch.append(pltpu.VMEM((ffw, d_model), jnp.float32))
    elif hidden is not None:
        out_specs.append(column)
        out_shape.append(jax.ShapeDtypeStruct((ffw, d_model), jnp.bfloat16))
    dots = (hidden is not None) + (gate_up is not None)
    return pl.pallas_call(
        functools.partial(
            phase_kernel, len(pieces), cut, wide, blocks, tall, grad is not None,
            0 if ready is None else 1, gate_up is not None, update,
        ),
        grid_spec=pltpu.PrefetchScalarGridSpec(
            num_scalar_prefetch=1,
            grid=(blocks + lines,),
            in_specs=specs,
            out_specs=out_specs,
            scratch_shapes=scratch,
        ),
        out_shape=out_shape,
        compiler_params=params,
        cost_estimate=pl.CostEstimate(
            flops=2 * dots * rows * ffw * d_model,
            bytes_accessed=8 * ffw * d_model,
            transcendentals=0,
        ),
    )(flags, *args)


def update_kernel(master_ref, *refs):
    update_rows(master_ref[0], [r[...].astype(jnp.float32) for r in refs[:-1]], refs[-1])


def update_call(master, grads):
    _, ffw, d_model = master.shape
    full = pl.BlockSpec((1, 128, d_model), lambda i: (0, i, 0))
    part = pl.BlockSpec((128, grads[0].shape[1]), lambda i: (i, 0))
    return pl.pallas_call(
        update_kernel,
        grid=(ffw // 128,),
        in_specs=[full] + [part] * len(grads),
        out_specs=full,
        out_shape=jax.ShapeDtypeStruct(master.shape, master.dtype),
        compiler_params=pltpu.CompilerParams(vmem_limit_bytes=20 * 2**20),
    )(master, *grads)


def after(value, other):
    return lax.optimization_barrier((value, other))[0]


def per_device(grad_out, gate_pre, up_pre, counts, placement, master):
    n_slot = lax.axis_size("expert")
    n_shard = lax.axis_size("shard")
    chips = n_shard // 2
    core = lax.axis_index("shard") % 2
    chip = lax.axis_index("shard") // 2
    slot = lax.axis_index("expert")
    rows, d_model = grad_out.shape[1:]
    order = jnp.arange(n_slot, dtype=jnp.int32)
    same = placement[:, None] == placement[None, :]
    pair_count = jnp.sum(same & (order[:, None] ^ 1 == order[None, :]), dtype=jnp.int32)
    four_count = jnp.sum(same & (order[:, None] ^ 2 == order[None, :]), dtype=jnp.int32)

    def share(bit):
        return jnp.any(same & (order[:, None] == slot) & (order[None, :] == slot ^ bit))

    orders = {}

    def send(value, axis, pairs):
        turn = orders.get((axis, *sorted(pairs)), 0)
        orders[(axis, *sorted(pairs))] = turn + 1
        turn, back = divmod(turn, 2)
        pairs = pairs[turn:] + pairs[:turn]
        return lax.ppermute(value, axis, pairs[::-1] if back else pairs)

    def to_slot(value, bit):
        return send(value, "expert", [(i, i ^ bit) for i in range(n_slot)])

    def to_core(value):
        return send(value, "shard", [(i, i ^ 1) for i in range(n_shard)])

    def to_chip(value, pairs):
        return send(value, "shard", [(2 * a + c, 2 * b + c) for a, b in pairs for c in range(2)])

    def along_chips(block, held=None):
        if chips != 4:
            return [block] + [
                to_chip(block, [((z + far) % chips, z) for z in range(chips)])
                for far in range(1, chips)
            ]
        two = to_chip(block, [(0, 2), (1, 3), (2, 0), (3, 1)])
        one = to_chip(block, [(1, 0), (2, 1), (3, 2)])
        three = to_chip(block, [(0, 1), (1, 2), (2, 3)])
        end = to_chip(two if held is None else after(two, held), [(2, 3), (1, 0)])
        one = jnp.where(chip == 3, end, one)
        three = jnp.where(chip == 0, end, three)
        return [block, one, two, three]

    def all_sum(grad, held):
        half = grad.shape[0] // 2
        done = []
        for part, bits in ((grad[:half], (1, 2)), (grad[half:], (2, 1))):
            sides = [jnp.where(slot & bit > 0, 1, 0) for bit in bits]
            for bit, side in zip(bits, sides):
                high = part.shape[0] // 2
                keep = lax.dynamic_slice_in_dim(part, side * high, high)
                send = lax.dynamic_slice_in_dim(part, (1 - side) * high, high)
                got = to_slot(send, bit)
                part = (keep.astype(jnp.float32) + got.astype(jnp.float32)).astype(part.dtype)
            part = after(part, held)
            for bit, side in zip(bits[::-1], sides[::-1]):
                got = to_slot(part, bit)
                part = jnp.concatenate(
                    [jnp.where(side == 0, part, got), jnp.where(side == 0, got, part)]
                )
            done.append(part)
        return jnp.concatenate(done)

    def body(mode, grad_out, gate_pre, up_pre, counts, placement, master):
        orders.clear()
        live = jnp.arange(rows, dtype=jnp.int32) < counts[0, 0]
        masked = jnp.where(live[:, None], grad_out[0], jnp.zeros((), grad_out.dtype))

        def gather(block):
            return lax.all_gather(block, "shard", axis=0, tiled=True)

        gate_up = (gate_pre, up_pre)
        if mode == "pair":
            width = d_model // 3
            early = to_slot(masked[:, 2 * width :], 1)
            hidden = hidden_transposed(gate_pre, up_pre)
            weight = weight_transposed(master)
            high = hidden.shape[0] // 2
            top = to_slot(after(hidden[:high], early), 1)
            low = to_slot(hidden[high:], 1)
            theirs = jnp.concatenate([top, low])
            one = gather(masked[:, :width])
            two = gather(after(masked[:, width:], (one, top, weight)))
            half = one.shape[0] // 2

            def to_partner(whole):
                return to_slot(lax.dynamic_slice(whole, (core * half, 0), (half, width)), 1)

            first = to_partner(one)
            rest = to_core(first)
            last = gather(after(early, (two, rest)))
            second = to_partner(two)
            flags = jnp.stack([share(1).astype(jnp.int32), core * half, (1 - core) * half])
            layout = [(0, None, 0, 0, width), (1, None, 0, width, 2 * width)]
            d_gate, d_up, grad = phase_call(
                flags, after([one, two], theirs), layout, hidden, gate_up=gate_up, weight=weight,
                d_model=d_model,
            )
            layout = [(0, None, (1,), 0, width), (1, None, (2,), 0, width)]
            ready = phase_call(
                flags, [first, rest], layout, theirs, grad=grad, d_model=width
            )[0]
            second = after(second, grad)
            layout = [
                (0, None, (1,), width, width),
                (1, None, (2,), width, width),
                (2, None, 0, 2 * width, width),
            ]
            fresh = phase_call(
                flags, [second, to_core(second), last], layout, theirs, master, grad=grad,
                ready=ready, update=True,
            )[0]
            return d_gate, d_up, fresh
        hidden = hidden_transposed(gate_pre, up_pre)
        weight = weight_transposed(master)
        flags = jnp.zeros((1,), jnp.int32)
        if mode == "none":
            layout = [(0, None, 0, 0, d_model)]
            return tuple(
                phase_call(
                    flags, [gather(masked)], layout, hidden, master, gate_up=gate_up,
                    weight=weight, update=True,
                )
            )
        width = d_model // 3
        wholes, grads = [], []
        for first in range(0, d_model, width):
            block = masked[:, first : first + width]
            wholes.append(gather(after(block, wholes[-1]) if wholes else block))
            layout = [(0, None, 0, 0, width)]
            grads.append(phase_call(flags, wholes[-1:], layout, hidden, d_model=width)[0])
        layout = [(i, None, 0, i * width, width) for i in range(3)]
        d_gate, d_up = phase_call(
            flags, wholes, layout, gate_up=gate_up, weight=weight, d_model=d_model
        )
        held = grads[1:] + [d_gate]
        for i, grad in enumerate(grads):
            if mode == "four":
                grads[i] = all_sum(grad, held[i])
                continue
            for bit in (1, 2):
                got = to_slot(grads[i], bit)
                grads[i] = grads[i] + jnp.where(share(bit), got, jnp.zeros((), got.dtype))
        return d_gate, d_up, update_call(master, grads)

    modes = ["none", "pair", "four"] + (["mixed"] if n_slot > 4 else [])
    mixed = jnp.where(four_count == n_slot, 2, len(modes) - 1)
    which = jnp.where(four_count > 0, mixed, jnp.where(pair_count > 0, 1, 0))
    return lax.switch(
        which,
        [lambda *a, mode=mode: body(mode, *a) for mode in modes],
        grad_out, gate_pre, up_pre, counts, placement, master,
    )


def solution(mesh):
    return jax.shard_map(
        per_device,
        mesh=mesh,
        in_specs=(
            P("expert", "shard", None),
            P("expert", None, "shard"),
            P("expert", None, "shard"),
            P("expert", "shard"),
            P(),
            P("expert", "shard", None),
        ),
        out_specs=(
            P("expert", None, "shard"),
            P("expert", None, "shard"),
            P("expert", "shard", None),
        ),
        check_vma=False,
    )
```

```python
import functools

import jax
import jax.numpy as jnp
from jax import lax
from jax.experimental import pallas as pl
from jax.experimental.pallas import tpu as pltpu
from jax.sharding import PartitionSpec as P

learn_rate = 0.02
rms_eps = 1e-06
tall = 256
params = pltpu.CompilerParams(vmem_limit_bytes=56 * 2**20)


def dot(a, b, dims):
    return lax.dot_general(a, b, (dims, ((), ())), preferred_element_type=jnp.float32)


def hidden_kernel(gate_ref, up_ref, out_ref):
    gate = gate_ref[0].astype(jnp.float32)
    hidden = gate * jax.nn.sigmoid(gate) * up_ref[0].astype(jnp.float32)
    out_ref[...] = hidden.T.astype(out_ref.dtype)


def hidden_transposed(gate_pre, up_pre):
    _, rows, ffw = gate_pre.shape
    block = pl.BlockSpec((1, tall, ffw), lambda i: (0, i, 0))
    return pl.pallas_call(
        hidden_kernel,
        grid=(rows // tall,),
        in_specs=[block, block],
        out_specs=pl.BlockSpec((ffw, tall), lambda i: (0, i)),
        out_shape=jax.ShapeDtypeStruct((ffw, rows), jnp.bfloat16),
        compiler_params=params,
    )(gate_pre, up_pre)


def weight_kernel(master_ref, out_ref):
    out_ref[...] = master_ref[0].astype(out_ref.dtype).T


def weight_transposed(master):
    _, ffw, d_model = master.shape
    return pl.pallas_call(
        weight_kernel,
        grid=(ffw // tall,),
        in_specs=[pl.BlockSpec((1, tall, d_model), lambda i: (0, i, 0))],
        out_specs=pl.BlockSpec((d_model, tall), lambda i: (0, i)),
        out_shape=jax.ShapeDtypeStruct((d_model, ffw), jnp.bfloat16),
        compiler_params=params,
        cost_estimate=pl.CostEstimate(
            flops=0, bytes_accessed=6 * ffw * d_model, transcendentals=0
        ),
    )(master)


def update_rows(master, grads, out_ref):
    square = sum(jnp.sum(g * g, axis=1, keepdims=True) for g in grads)
    scale = learn_rate / jnp.sqrt(square / master.shape[1] + rms_eps)
    first = 0
    for grad in grads:
        cols = slice(first, first + grad.shape[1])
        out_ref[0, :, cols] = master[:, cols] - grad * scale
        first += grad.shape[1]


def gates_back(d_hidden, gate_ref, up_ref, gate_out, up_out):
    gate = gate_ref[0].astype(jnp.float32)
    up = up_ref[0].astype(jnp.float32)
    sig = jax.nn.sigmoid(gate)
    up_out[0] = (d_hidden * (gate * sig)).astype(up_out.dtype)
    slope = sig * (1.0 + gate * (1.0 - sig))
    gate_out[0] = (d_hidden * up * slope).astype(gate_out.dtype)


def phase_kernel(n_pieces, layout, wide, blocks, tall, grad_in, ready, gates, update, flag_ref,
                 *refs):
    refs = list(refs)
    pieces = [refs.pop(0) for _ in range(n_pieces)]
    hidden_ref = refs.pop(0) if blocks else None
    master_hbm = refs.pop(0) if update else None
    grad_ref = refs.pop(0) if grad_in else None
    ready_ref = refs.pop(0) if ready else None
    weight_ref, gate_ref, up_ref = [refs.pop(0) if gates else None for _ in range(3)]
    gate_out, up_out = (refs.pop(0), refs.pop(0)) if gates else (None, None)
    out_ref = refs.pop(0) if blocks else None
    whole_ref, sem_ref = refs[:2]
    master_ref, master_sem = refs[2:4] if update else (None, None)
    sum_ref = refs[4] if update else None
    step = pl.program_id(0)
    by_block = {}
    for place, (ref, index, row, source_first, first, count) in enumerate(layout):
        source = pieces[ref] if index is None else pieces[ref].at[index]
        high = source.shape[0]
        start = row if isinstance(row, int) else pl.multiple_of(flag_ref[row[0]], 128)
        copy = pltpu.make_async_copy(
            source.at[:, pl.ds(source_first, count)],
            whole_ref.at[pl.ds(start, high), pl.ds(first, count)],
            sem_ref.at[place],
        )
        by_block.setdefault(first // wide, []).append(copy)
    master_copies = []
    if update:
        for i in range(master_ref.shape[0] // tall):
            lines = pl.ds(i * tall, tall)
            master_copies.append(
                pltpu.make_async_copy(
                    master_hbm.at[0, lines], master_ref.at[lines], master_sem.at[i]
                )
            )

    @pl.when(step == 0)
    def _():
        for block in sorted(by_block):
            for copy in by_block[block]:
                copy.start()
        for copy in master_copies:
            copy.start()

    for block in sorted(by_block):

        @pl.when(step == min(block, blocks))
        def _(block=block):
            for copy in by_block[block]:
                copy.wait()

    for i, copy in enumerate(master_copies):

        @pl.when(step == blocks + i)
        def _(copy=copy):
            copy.wait()

    if ready:

        @pl.when(step == 0)
        def _():
            sum_ref[:, :wide] = ready_ref[...].astype(jnp.float32)

    if blocks:

        @pl.when((step >= ready) & (step < blocks))
        def _():
            cols = pl.ds(pl.multiple_of(step * wide, wide), wide)
            grad = dot(hidden_ref[...], whole_ref[:, cols], ((1,), (0,)))
            if grad_in:
                own = grad_ref[...].astype(jnp.float32)
                grad = own + jnp.where(flag_ref[0] > 0, grad, 0.0)
            if update:
                sum_ref[:, cols] = grad
            else:
                out_ref[...] = grad.astype(out_ref.dtype)

    if gates or update:

        @pl.when(step >= blocks)
        def _():
            lines = pl.ds(pl.multiple_of((step - blocks) * tall, tall), tall)
            if update:
                update_rows(master_ref[lines, :], [sum_ref[lines, :]], out_ref)
            if gates:
                d_hidden = dot(whole_ref[...], weight_ref[...], ((1,), (0,)))
                gates_back(d_hidden, gate_ref, up_ref, gate_out, up_out)


def phase_call(flags, pieces, layout, hidden=None, master=None, grad=None, gate_up=None,
               weight=None, ready=None, update=False, d_model=None):
    ffw = hidden.shape[0] if gate_up is None else gate_up[0].shape[2]
    if master is not None:
        d_model = master.shape[2]
    rows = gate_up[0].shape[1] if hidden is None else hidden.shape[1]
    wide = next(w for w in (1024, 768, 512, 128) if d_model % w == 0)
    blocks = d_model // wide if hidden is not None else 0
    lines = ffw // tall if update or gate_up is not None else 0
    cut = []
    for ref, index, row, first, count in layout:
        piece = wide if blocks else count
        for at in range(0, count, piece):
            cut.append((ref, index, row, at, first + at, piece))
    row_block = lambda i: jnp.maximum(i - blocks, 0)
    col_block = lambda i: jnp.minimum(i, blocks - 1)
    anywhere = pl.BlockSpec(memory_space=pl.ANY)
    side = pl.BlockSpec((1, rows, tall), lambda i, flag: (0, 0, row_block(i)))
    full = pl.BlockSpec((1, tall, d_model), lambda i, flag: (0, row_block(i), 0))
    column = pl.BlockSpec((ffw, wide), lambda i, flag: (0, col_block(i)))
    specs, args = [anywhere] * len(pieces), list(pieces)
    out_specs, out_shape = [], []
    scratch = [
        pltpu.VMEM((rows, d_model), jnp.bfloat16),
        pltpu.SemaphoreType.DMA((len(cut),)),
    ]
    if hidden is not None:
        specs.append(pl.BlockSpec((ffw, rows), lambda i, flag: (0, 0), pipeline_mode=pl.Buffered(1)))
        args.append(hidden)
    if master is not None:
        specs.append(anywhere)
        args.append(master)
        scratch.append(pltpu.VMEM((ffw, d_model), jnp.float32))
        scratch.append(pltpu.SemaphoreType.DMA((lines,)))
    if grad is not None:
        specs.append(column)
        args.append(grad)
    if ready is not None:
        specs.append(pl.BlockSpec((ffw, wide), lambda i, flag: (0, 0)))
        args.append(ready)
    if gate_up is not None:
        specs += [pl.BlockSpec((d_model, tall), lambda i, flag: (0, row_block(i))), side, side]
        args += [weight, *gate_up]
        out_specs += [side, side]
        out_shape += [jax.ShapeDtypeStruct(a.shape, a.dtype) for a in gate_up]
    if update:
        out_specs.append(full)
        out_shape.append(jax.ShapeDtypeStruct(master.shape, master.dtype))
        scratch.append(pltpu.VMEM((ffw, d_model), jnp.float32))
    elif hidden is not None:
        out_specs.append(column)
        out_shape.append(jax.ShapeDtypeStruct((ffw, d_model), jnp.bfloat16))
    dots = (hidden is not None) + (gate_up is not None)
    return pl.pallas_call(
        functools.partial(
            phase_kernel, len(pieces), cut, wide, blocks, tall, grad is not None,
            0 if ready is None else 1, gate_up is not None, update,
        ),
        grid_spec=pltpu.PrefetchScalarGridSpec(
            num_scalar_prefetch=1,
            grid=(blocks + lines,),
            in_specs=specs,
            out_specs=out_specs,
            scratch_shapes=scratch,
        ),
        out_shape=out_shape,
        compiler_params=params,
        cost_estimate=pl.CostEstimate(
            flops=2 * dots * rows * ffw * d_model,
            bytes_accessed=8 * ffw * d_model,
            transcendentals=0,
        ),
    )(flags, *args)


def update_kernel(master_ref, *refs):
    update_rows(master_ref[0], [r[...].astype(jnp.float32) for r in refs[:-1]], refs[-1])


def update_call(master, grads):
    _, ffw, d_model = master.shape
    full = pl.BlockSpec((1, 128, d_model), lambda i: (0, i, 0))
    part = pl.BlockSpec((128, grads[0].shape[1]), lambda i: (i, 0))
    return pl.pallas_call(
        update_kernel,
        grid=(ffw // 128,),
        in_specs=[full] + [part] * len(grads),
        out_specs=full,
        out_shape=jax.ShapeDtypeStruct(master.shape, master.dtype),
        compiler_params=pltpu.CompilerParams(vmem_limit_bytes=20 * 2**20),
    )(master, *grads)


def after(value, other):
    return lax.optimization_barrier((value, other))[0]


def per_device(grad_out, gate_pre, up_pre, counts, placement, master):
    n_slot = lax.axis_size("expert")
    n_shard = lax.axis_size("shard")
    chips = n_shard // 2
    core = lax.axis_index("shard") % 2
    chip = lax.axis_index("shard") // 2
    slot = lax.axis_index("expert")
    rows, d_model = grad_out.shape[1:]
    order = jnp.arange(n_slot, dtype=jnp.int32)
    same = placement[:, None] == placement[None, :]
    pair_count = jnp.sum(same & (order[:, None] ^ 1 == order[None, :]), dtype=jnp.int32)
    four_count = jnp.sum(same & (order[:, None] ^ 2 == order[None, :]), dtype=jnp.int32)

    def share(bit):
        return jnp.any(same & (order[:, None] == slot) & (order[None, :] == slot ^ bit))

    orders = {}

    def send(value, axis, pairs):
        turn = orders.get((axis, *sorted(pairs)), 0)
        orders[(axis, *sorted(pairs))] = turn + 1
        turn, back = divmod(turn, 2)
        pairs = pairs[turn:] + pairs[:turn]
        return lax.ppermute(value, axis, pairs[::-1] if back else pairs)

    def to_slot(value, bit):
        return send(value, "expert", [(i, i ^ bit) for i in range(n_slot)])

    def to_core(value):
        return send(value, "shard", [(i, i ^ 1) for i in range(n_shard)])

    def to_chip(value, pairs):
        return send(value, "shard", [(2 * a + c, 2 * b + c) for a, b in pairs for c in range(2)])

    def along_chips(block, held=None):
        if chips != 4:
            return [block] + [
                to_chip(block, [((z + far) % chips, z) for z in range(chips)])
                for far in range(1, chips)
            ]
        two = to_chip(block, [(0, 2), (1, 3), (2, 0), (3, 1)])
        one = to_chip(block, [(1, 0), (2, 1), (3, 2)])
        three = to_chip(block, [(0, 1), (1, 2), (2, 3)])
        end = to_chip(two if held is None else after(two, held), [(2, 3), (1, 0)])
        one = jnp.where(chip == 3, end, one)
        three = jnp.where(chip == 0, end, three)
        return [block, one, two, three]

    def all_sum(grad, held):
        half = grad.shape[0] // 2
        done = []
        for part, bits in ((grad[:half], (1, 2)), (grad[half:], (2, 1))):
            sides = [jnp.where(slot & bit > 0, 1, 0) for bit in bits]
            for bit, side in zip(bits, sides):
                high = part.shape[0] // 2
                keep = lax.dynamic_slice_in_dim(part, side * high, high)
                send = lax.dynamic_slice_in_dim(part, (1 - side) * high, high)
                got = to_slot(send, bit)
                part = (keep.astype(jnp.float32) + got.astype(jnp.float32)).astype(part.dtype)
            part = after(part, held)
            for bit, side in zip(bits[::-1], sides[::-1]):
                got = to_slot(part, bit)
                part = jnp.concatenate(
                    [jnp.where(side == 0, part, got), jnp.where(side == 0, got, part)]
                )
            done.append(part)
        return jnp.concatenate(done)

    def body(mode, grad_out, gate_pre, up_pre, counts, placement, master):
        orders.clear()
        live = jnp.arange(rows, dtype=jnp.int32) < counts[0, 0]
        masked = jnp.where(live[:, None], grad_out[0], jnp.zeros((), grad_out.dtype))

        def gather(block):
            return lax.all_gather(block, "shard", axis=0, tiled=True)

        gate_up = (gate_pre, up_pre)
        if mode == "pair":
            width = d_model // 3
            early = to_slot(masked[:, 2 * width :], 1)
            hidden = hidden_transposed(gate_pre, up_pre)
            weight = weight_transposed(master)
            high = hidden.shape[0] // 2
            top = to_slot(after(hidden[:high], early), 1)
            low = to_slot(hidden[high:], 1)
            theirs = jnp.concatenate([top, low])
            one = gather(masked[:, :width])
            two = gather(after(masked[:, width:], (one, top, weight)))
            half = one.shape[0] // 2

            def to_partner(whole):
                return to_slot(lax.dynamic_slice(whole, (core * half, 0), (half, width)), 1)

            first = to_partner(one)
            rest = to_core(first)
            last = gather(after(early, (two, rest, low)))
            second = to_partner(two)
            flags = jnp.stack([share(1).astype(jnp.int32), core * half, (1 - core) * half])
            layout = [(0, None, 0, 0, width), (1, None, 0, width, 2 * width)]
            d_gate, d_up, grad = phase_call(
                flags, after([one, two], theirs), layout, hidden, gate_up=gate_up, weight=weight,
                d_model=d_model,
            )
            second = after(second, grad)
            layout = [
                (0, None, (1,), 0, width),
                (1, None, (2,), 0, width),
                (2, None, (1,), width, width),
                (3, None, (2,), width, width),
                (4, None, 0, 2 * width, width),
            ]
            fresh = phase_call(
                flags, [first, rest, second, to_core(second), last], layout, theirs, master,
                grad=grad, update=True,
            )[0]
            return d_gate, d_up, fresh
        hidden = hidden_transposed(gate_pre, up_pre)
        weight = weight_transposed(master)
        flags = jnp.zeros((1,), jnp.int32)
        if mode == "none":
            layout = [(0, None, 0, 0, d_model)]
            return tuple(
                phase_call(
                    flags, [gather(masked)], layout, hidden, master, gate_up=gate_up,
                    weight=weight, update=True,
                )
            )
        width = d_model // 3
        wholes, grads = [], []
        for first in range(0, d_model, width):
            block = masked[:, first : first + width]
            if wholes:
                block = after(block, (wholes[-1], hidden, weight))
            wholes.append(gather(block))
            layout = [(0, None, 0, 0, width)]
            grads.append(phase_call(flags, wholes[-1:], layout, hidden, d_model=width)[0])
        layout = [(i, None, 0, i * width, width) for i in range(3)]
        d_gate, d_up = phase_call(
            flags, wholes, layout, gate_up=gate_up, weight=weight, d_model=d_model
        )
        held = grads[1:] + [d_gate]
        for i, grad in enumerate(grads):
            if mode == "four":
                grads[i] = all_sum(grad, held[i])
                continue
            for bit in (1, 2):
                got = to_slot(grads[i], bit)
                grads[i] = grads[i] + jnp.where(share(bit), got, jnp.zeros((), got.dtype))
        return d_gate, d_up, update_call(master, grads)

    modes = ["none", "pair", "four"] + (["mixed"] if n_slot > 4 else [])
    mixed = jnp.where(four_count == n_slot, 2, len(modes) - 1)
    which = jnp.where(four_count > 0, mixed, jnp.where(pair_count > 0, 1, 0))
    return lax.switch(
        which,
        [lambda *a, mode=mode: body(mode, *a) for mode in modes],
        grad_out, gate_pre, up_pre, counts, placement, master,
    )


def solution(mesh):
    return jax.shard_map(
        per_device,
        mesh=mesh,
        in_specs=(
            P("expert", "shard", None),
            P("expert", None, "shard"),
            P("expert", None, "shard"),
            P("expert", "shard"),
            P(),
            P("expert", "shard", None),
        ),
        out_specs=(
            P("expert", None, "shard"),
            P("expert", None, "shard"),
            P("expert", "shard", None),
        ),
        check_vma=False,
    )
```

```python
import functools

import jax
import jax.numpy as jnp
from jax import lax
from jax.experimental import pallas as pl
from jax.experimental.pallas import tpu as pltpu
from jax.sharding import PartitionSpec as P

learn_rate = 0.02
rms_eps = 1e-06
tall = 256
params = pltpu.CompilerParams(vmem_limit_bytes=56 * 2**20)


def dot(a, b, dims):
    return lax.dot_general(a, b, (dims, ((), ())), preferred_element_type=jnp.float32)


def hidden_kernel(gate_ref, up_ref, out_ref):
    gate = gate_ref[0].astype(jnp.float32)
    hidden = gate * jax.nn.sigmoid(gate) * up_ref[0].astype(jnp.float32)
    out_ref[...] = hidden.T.astype(out_ref.dtype)


def hidden_transposed(gate_pre, up_pre):
    _, rows, ffw = gate_pre.shape
    block = pl.BlockSpec((1, tall, ffw), lambda i: (0, i, 0))
    return pl.pallas_call(
        hidden_kernel,
        grid=(rows // tall,),
        in_specs=[block, block],
        out_specs=pl.BlockSpec((ffw, tall), lambda i: (0, i)),
        out_shape=jax.ShapeDtypeStruct((ffw, rows), jnp.bfloat16),
        compiler_params=params,
    )(gate_pre, up_pre)


def weight_kernel(master_ref, out_ref):
    out_ref[...] = master_ref[0].astype(out_ref.dtype).T


def weight_transposed(master):
    _, ffw, d_model = master.shape
    return pl.pallas_call(
        weight_kernel,
        grid=(ffw // tall,),
        in_specs=[pl.BlockSpec((1, tall, d_model), lambda i: (0, i, 0))],
        out_specs=pl.BlockSpec((d_model, tall), lambda i: (0, i)),
        out_shape=jax.ShapeDtypeStruct((d_model, ffw), jnp.bfloat16),
        compiler_params=params,
        cost_estimate=pl.CostEstimate(
            flops=0, bytes_accessed=6 * ffw * d_model, transcendentals=0
        ),
    )(master)


def update_rows(master, grads, out_ref):
    square = sum(jnp.sum(g * g, axis=1, keepdims=True) for g in grads)
    scale = learn_rate / jnp.sqrt(square / master.shape[1] + rms_eps)
    first = 0
    for grad in grads:
        cols = slice(first, first + grad.shape[1])
        out_ref[0, :, cols] = master[:, cols] - grad * scale
        first += grad.shape[1]


def gates_back(d_hidden, gate_ref, up_ref, gate_out, up_out):
    gate = gate_ref[0].astype(jnp.float32)
    up = up_ref[0].astype(jnp.float32)
    sig = jax.nn.sigmoid(gate)
    up_out[0] = (d_hidden * (gate * sig)).astype(up_out.dtype)
    slope = sig * (1.0 + gate * (1.0 - sig))
    gate_out[0] = (d_hidden * up * slope).astype(gate_out.dtype)


def phase_kernel(n_pieces, layout, wide, blocks, tall, grad_in, ready, gates, update, flag_ref,
                 *refs):
    refs = list(refs)
    pieces = [refs.pop(0) for _ in range(n_pieces)]
    hidden_ref = refs.pop(0) if blocks else None
    master_hbm = refs.pop(0) if update else None
    grad_ref = refs.pop(0) if grad_in else None
    ready_ref = refs.pop(0) if ready else None
    weight_ref, gate_ref, up_ref = [refs.pop(0) if gates else None for _ in range(3)]
    gate_out, up_out = (refs.pop(0), refs.pop(0)) if gates else (None, None)
    out_ref = refs.pop(0) if blocks else None
    whole_ref, sem_ref = refs[:2]
    master_ref, master_sem = refs[2:4] if update else (None, None)
    sum_ref = refs[4] if update else None
    step = pl.program_id(0)
    by_block = {}
    for place, (ref, index, row, source_first, first, count) in enumerate(layout):
        source = pieces[ref] if index is None else pieces[ref].at[index]
        high = source.shape[0]
        start = row if isinstance(row, int) else pl.multiple_of(flag_ref[row[0]], 128)
        copy = pltpu.make_async_copy(
            source.at[:, pl.ds(source_first, count)],
            whole_ref.at[pl.ds(start, high), pl.ds(first, count)],
            sem_ref.at[place],
        )
        by_block.setdefault(first // wide, []).append(copy)
    master_copies = []
    if update:
        for i in range(master_ref.shape[0] // tall):
            lines = pl.ds(i * tall, tall)
            master_copies.append(
                pltpu.make_async_copy(
                    master_hbm.at[0, lines], master_ref.at[lines], master_sem.at[i]
                )
            )

    @pl.when(step == 0)
    def _():
        for block in sorted(by_block):
            for copy in by_block[block]:
                copy.start()
        for copy in master_copies:
            copy.start()

    for block in sorted(by_block):

        @pl.when(step == min(block, blocks))
        def _(block=block):
            for copy in by_block[block]:
                copy.wait()

    for i, copy in enumerate(master_copies):

        @pl.when(step == blocks + i)
        def _(copy=copy):
            copy.wait()

    if ready:

        @pl.when(step == 0)
        def _():
            sum_ref[:, :wide] = ready_ref[...].astype(jnp.float32)

    if blocks:

        @pl.when((step >= ready) & (step < blocks))
        def _():
            cols = pl.ds(pl.multiple_of(step * wide, wide), wide)
            grad = dot(hidden_ref[...], whole_ref[:, cols], ((1,), (0,)))
            if grad_in:
                own = grad_ref[...].astype(jnp.float32)
                grad = own + jnp.where(flag_ref[0] > 0, grad, 0.0)
            if update:
                sum_ref[:, cols] = grad
            else:
                out_ref[...] = grad.astype(out_ref.dtype)

    if gates or update:

        @pl.when(step >= blocks)
        def _():
            lines = pl.ds(pl.multiple_of((step - blocks) * tall, tall), tall)
            if update:
                update_rows(master_ref[lines, :], [sum_ref[lines, :]], out_ref)
            if gates:
                d_hidden = dot(whole_ref[...], weight_ref[...], ((1,), (0,)))
                gates_back(d_hidden, gate_ref, up_ref, gate_out, up_out)


def phase_call(flags, pieces, layout, hidden=None, master=None, grad=None, gate_up=None,
               weight=None, ready=None, update=False, d_model=None):
    ffw = hidden.shape[0] if gate_up is None else gate_up[0].shape[2]
    if master is not None:
        d_model = master.shape[2]
    rows = gate_up[0].shape[1] if hidden is None else hidden.shape[1]
    wide = next(w for w in (1024, 768, 512, 128) if d_model % w == 0)
    blocks = d_model // wide if hidden is not None else 0
    lines = ffw // tall if update or gate_up is not None else 0
    cut = []
    for ref, index, row, first, count in layout:
        piece = wide if blocks else count
        for at in range(0, count, piece):
            cut.append((ref, index, row, at, first + at, piece))
    row_block = lambda i: jnp.maximum(i - blocks, 0)
    col_block = lambda i: jnp.minimum(i, blocks - 1)
    anywhere = pl.BlockSpec(memory_space=pl.ANY)
    side = pl.BlockSpec((1, rows, tall), lambda i, flag: (0, 0, row_block(i)))
    full = pl.BlockSpec((1, tall, d_model), lambda i, flag: (0, row_block(i), 0))
    column = pl.BlockSpec((ffw, wide), lambda i, flag: (0, col_block(i)))
    specs, args = [anywhere] * len(pieces), list(pieces)
    out_specs, out_shape = [], []
    scratch = [
        pltpu.VMEM((rows, d_model), jnp.bfloat16),
        pltpu.SemaphoreType.DMA((len(cut),)),
    ]
    if hidden is not None:
        specs.append(pl.BlockSpec((ffw, rows), lambda i, flag: (0, 0), pipeline_mode=pl.Buffered(1)))
        args.append(hidden)
    if master is not None:
        specs.append(anywhere)
        args.append(master)
        scratch.append(pltpu.VMEM((ffw, d_model), jnp.float32))
        scratch.append(pltpu.SemaphoreType.DMA((lines,)))
    if grad is not None:
        specs.append(column)
        args.append(grad)
    if ready is not None:
        specs.append(pl.BlockSpec((ffw, wide), lambda i, flag: (0, 0)))
        args.append(ready)
    if gate_up is not None:
        specs += [pl.BlockSpec((d_model, tall), lambda i, flag: (0, row_block(i))), side, side]
        args += [weight, *gate_up]
        out_specs += [side, side]
        out_shape += [jax.ShapeDtypeStruct(a.shape, a.dtype) for a in gate_up]
    if update:
        out_specs.append(full)
        out_shape.append(jax.ShapeDtypeStruct(master.shape, master.dtype))
        scratch.append(pltpu.VMEM((ffw, d_model), jnp.float32))
    elif hidden is not None:
        out_specs.append(column)
        out_shape.append(jax.ShapeDtypeStruct((ffw, d_model), jnp.bfloat16))
    dots = (hidden is not None) + (gate_up is not None)
    return pl.pallas_call(
        functools.partial(
            phase_kernel, len(pieces), cut, wide, blocks, tall, grad is not None,
            0 if ready is None else 1, gate_up is not None, update,
        ),
        grid_spec=pltpu.PrefetchScalarGridSpec(
            num_scalar_prefetch=1,
            grid=(blocks + lines,),
            in_specs=specs,
            out_specs=out_specs,
            scratch_shapes=scratch,
        ),
        out_shape=out_shape,
        compiler_params=params,
        cost_estimate=pl.CostEstimate(
            flops=2 * dots * rows * ffw * d_model,
            bytes_accessed=8 * ffw * d_model,
            transcendentals=0,
        ),
    )(flags, *args)


def update_kernel(master_ref, *refs):
    update_rows(master_ref[0], [r[...].astype(jnp.float32) for r in refs[:-1]], refs[-1])


def update_call(master, grads):
    _, ffw, d_model = master.shape
    full = pl.BlockSpec((1, 128, d_model), lambda i: (0, i, 0))
    part = pl.BlockSpec((128, grads[0].shape[1]), lambda i: (i, 0))
    return pl.pallas_call(
        update_kernel,
        grid=(ffw // 128,),
        in_specs=[full] + [part] * len(grads),
        out_specs=full,
        out_shape=jax.ShapeDtypeStruct(master.shape, master.dtype),
        compiler_params=pltpu.CompilerParams(vmem_limit_bytes=20 * 2**20),
    )(master, *grads)


def after(value, other):
    return lax.optimization_barrier((value, other))[0]


def per_device(grad_out, gate_pre, up_pre, counts, placement, master):
    n_slot = lax.axis_size("expert")
    n_shard = lax.axis_size("shard")
    chips = n_shard // 2
    core = lax.axis_index("shard") % 2
    chip = lax.axis_index("shard") // 2
    slot = lax.axis_index("expert")
    rows, d_model = grad_out.shape[1:]
    order = jnp.arange(n_slot, dtype=jnp.int32)
    same = placement[:, None] == placement[None, :]
    pair_count = jnp.sum(same & (order[:, None] ^ 1 == order[None, :]), dtype=jnp.int32)
    four_count = jnp.sum(same & (order[:, None] ^ 2 == order[None, :]), dtype=jnp.int32)

    def share(bit):
        return jnp.any(same & (order[:, None] == slot) & (order[None, :] == slot ^ bit))

    orders = {}

    def send(value, axis, pairs):
        turn = orders.get((axis, *sorted(pairs)), 0)
        orders[(axis, *sorted(pairs))] = turn + 1
        turn, back = divmod(turn, 2)
        pairs = pairs[turn:] + pairs[:turn]
        return lax.ppermute(value, axis, pairs[::-1] if back else pairs)

    def to_slot(value, bit):
        return send(value, "expert", [(i, i ^ bit) for i in range(n_slot)])

    def to_core(value):
        return send(value, "shard", [(i, i ^ 1) for i in range(n_shard)])

    def to_chip(value, pairs):
        return send(value, "shard", [(2 * a + c, 2 * b + c) for a, b in pairs for c in range(2)])

    def along_chips(block, held=None):
        if chips != 4:
            return [block] + [
                to_chip(block, [((z + far) % chips, z) for z in range(chips)])
                for far in range(1, chips)
            ]
        two = to_chip(block, [(0, 2), (1, 3), (2, 0), (3, 1)])
        one = to_chip(block, [(1, 0), (2, 1), (3, 2)])
        three = to_chip(block, [(0, 1), (1, 2), (2, 3)])
        end = to_chip(two if held is None else after(two, held), [(2, 3), (1, 0)])
        one = jnp.where(chip == 3, end, one)
        three = jnp.where(chip == 0, end, three)
        return [block, one, two, three]

    def all_sum(grad, held):
        half = grad.shape[0] // 2
        done = []
        for part, bits in ((grad[:half], (1, 2)), (grad[half:], (2, 1))):
            sides = [jnp.where(slot & bit > 0, 1, 0) for bit in bits]
            for bit, side in zip(bits, sides):
                high = part.shape[0] // 2
                keep = lax.dynamic_slice_in_dim(part, side * high, high)
                send = lax.dynamic_slice_in_dim(part, (1 - side) * high, high)
                got = to_slot(send, bit)
                part = (keep.astype(jnp.float32) + got.astype(jnp.float32)).astype(part.dtype)
            part = after(part, held)
            for bit, side in zip(bits[::-1], sides[::-1]):
                got = to_slot(part, bit)
                part = jnp.concatenate(
                    [jnp.where(side == 0, part, got), jnp.where(side == 0, got, part)]
                )
            done.append(part)
        return jnp.concatenate(done)

    def body(mode, grad_out, gate_pre, up_pre, counts, placement, master):
        orders.clear()
        live = jnp.arange(rows, dtype=jnp.int32) < counts[0, 0]
        masked = jnp.where(live[:, None], grad_out[0], jnp.zeros((), grad_out.dtype))

        def gather(block):
            return lax.all_gather(block, "shard", axis=0, tiled=True)

        gate_up = (gate_pre, up_pre)
        if mode == "pair":
            width = d_model // 3
            early = to_slot(masked[:, 2 * width :], 1)
            hidden = hidden_transposed(gate_pre, up_pre)
            weight = weight_transposed(master)
            high = hidden.shape[0] // 2
            half = hidden.shape[1] // 2
            flags = jnp.stack([share(1).astype(jnp.int32), core * half, (1 - core) * half])
            top = to_slot(after(hidden[:high], (early, flags)), 1)
            low = to_slot(hidden[high:], 1)
            theirs = jnp.concatenate([top, low])
            one = gather(masked[:, :width])
            two = gather(after(masked[:, width:], (one, top, weight)))

            def to_partner(whole):
                return to_slot(lax.dynamic_slice(whole, (core * half, 0), (half, width)), 1)

            first = to_partner(one)
            rest = to_core(first)
            last = gather(after(early, (two, rest, low)))
            second = to_partner(two)
            layout = [(0, None, 0, 0, width), (1, None, 0, width, 2 * width)]
            d_gate, d_up, grad = phase_call(
                flags, after([one, two], theirs), layout, hidden, gate_up=gate_up, weight=weight,
                d_model=d_model,
            )
            second = after(second, grad)
            layout = [
                (0, None, (1,), 0, width),
                (1, None, (2,), 0, width),
                (2, None, (1,), width, width),
                (3, None, (2,), width, width),
                (4, None, 0, 2 * width, width),
            ]
            fresh = phase_call(
                flags, [first, rest, second, to_core(second), last], layout, theirs, master,
                grad=grad, update=True,
            )[0]
            return d_gate, d_up, fresh
        hidden = hidden_transposed(gate_pre, up_pre)
        weight = weight_transposed(master)
        flags = jnp.zeros((1,), jnp.int32)
        if mode == "none":
            layout = [(0, None, 0, 0, d_model)]
            return tuple(
                phase_call(
                    flags, [gather(masked)], layout, hidden, master, gate_up=gate_up,
                    weight=weight, update=True,
                )
            )
        width = d_model // 3
        wholes, grads = [], []
        for first in range(0, d_model, width):
            block = masked[:, first : first + width]
            if wholes:
                block = after(block, (wholes[-1], hidden, weight))
            wholes.append(gather(block))
            layout = [(0, None, 0, 0, width)]
            grads.append(phase_call(flags, wholes[-1:], layout, hidden, d_model=width)[0])
        layout = [(i, None, 0, i * width, width) for i in range(3)]
        d_gate, d_up = phase_call(
            flags, wholes, layout, gate_up=gate_up, weight=weight, d_model=d_model
        )
        held = grads[1:] + [d_gate]
        for i, grad in enumerate(grads):
            if mode == "four":
                grads[i] = all_sum(grad, held[i])
                continue
            for bit in (1, 2):
                got = to_slot(grads[i], bit)
                grads[i] = grads[i] + jnp.where(share(bit), got, jnp.zeros((), got.dtype))
        return d_gate, d_up, update_call(master, grads)

    modes = ["none", "pair", "four"] + (["mixed"] if n_slot > 4 else [])
    mixed = jnp.where(four_count == n_slot, 2, len(modes) - 1)
    which = jnp.where(four_count > 0, mixed, jnp.where(pair_count > 0, 1, 0))
    return lax.switch(
        which,
        [lambda *a, mode=mode: body(mode, *a) for mode in modes],
        grad_out, gate_pre, up_pre, counts, placement, master,
    )


def solution(mesh):
    return jax.shard_map(
        per_device,
        mesh=mesh,
        in_specs=(
            P("expert", "shard", None),
            P("expert", None, "shard"),
            P("expert", None, "shard"),
            P("expert", "shard"),
            P(),
            P("expert", "shard", None),
        ),
        out_specs=(
            P("expert", None, "shard"),
            P("expert", None, "shard"),
            P("expert", "shard", None),
        ),
        check_vma=False,
    )
```
